512 devices in a mesh: ctx: 16 (over z), sec: 4 (over y_hi, core), tp: 8 (over x, y_lo).
Axes of the slice: x: 4, y: 4 (y_hi: 2, y_lo: 2; y = y_hi * 2 + y_lo), z: 16, core: 2. Of those that a mesh axis runs over, the one named last changes fastest.
Arguments:
- prompt_query: bfloat16 [8192, 8, 8, 128], P('ctx', 'tp', 'sec'), may hold values from -250 to 250
- prompt_keys: bfloat16 [8192, 8, 128], P(('ctx', 'sec'), 'tp'), may hold values from -6 to 6
- prompt_values: bfloat16 [8192, 8, 128], P(('ctx', 'sec'), 'tp'), may hold values from -6 to 6
- decode_query: bfloat16 [1024, 4, 8, 8, 128], P(('ctx', 'sec', 'tp')), may hold values from -250 to 250
- new_keys: bfloat16 [1024, 4, 8, 128], P(('ctx', 'sec', 'tp')), may hold values from -6 to 6
- new_values: bfloat16 [1024, 4, 8, 128], P(('ctx', 'sec', 'tp')), may hold values from -6 to 6
- cache_keys: bfloat16 [1024, 256, 8, 128], P(('ctx', 'sec'), None, 'tp'), may hold values from -6 to 6
- cache_values: bfloat16 [1024, 256, 8, 128], P(('ctx', 'sec'), None, 'tp'), may hold values from -6 to 6
- cache_len: int32 [1024], P(('ctx', 'sec')), may hold values from 1 to 256, as said below
Outputs:
- prompt_attn: bfloat16 [8192, 8, 8, 128], P('ctx', 'tp', 'sec')
- decoded: bfloat16 [1024, 4, 8, 8, 128], P(('ctx', 'sec', 'tp'))
The draws below stay inside these ranges and needn't reach their ends.
Inputs may be any that keep to these rules, and one draw needn't show every extreme that they name: Row r sees the first cache_len[r] of its 256 cache slots; some row has all 256.
All inputs are finite; a program needn't handle non-finite values.
Results may differ from the reference program's by a relative error of at most 0.009.
Values may be sent and summed in bfloat16 or wider, within the bound.
A program may use at most 64 MiB of HBM per device.

```python
import math
import jax
import jax.numpy as jnp
from jax import lax

D_HEAD = 128
KV_HEADS = 8
GROUP = 8
CACHE = 256
STEPS = 4
PROMPT = 8192
NROWS = 1024


def prompt_base(key):
    raw = jax.random.normal(jax.random.fold_in(key, 101), (PROMPT, KV_HEADS, D_HEAD), jnp.float32)
    return jnp.clip(raw, -6.0, 6.0)


def fresh_base(key):
    raw = jax.random.normal(jax.random.fold_in(key, 202), (NROWS, STEPS, KV_HEADS, D_HEAD), jnp.float32)
    return jnp.clip(raw, -6.0, 6.0)


def draw_prompt_keys(key, part):
    return prompt_base(key).astype(jnp.bfloat16)


def draw_prompt_query(key, part):
    key = jax.random.fold_in(key, 3)
    drawn = jnp.clip(jax.random.normal(key, (PROMPT, KV_HEADS, GROUP, D_HEAD), jnp.float32), -6.0, 6.0)
    return drawn.astype(jnp.bfloat16)


def draw_new_keys(key, part):
    return fresh_base(key).astype(jnp.bfloat16)


def draw_decode_query(key, part):
    key = jax.random.fold_in(key, 4)
    drawn = jnp.clip(jax.random.normal(key, (NROWS, STEPS, KV_HEADS, GROUP, D_HEAD), jnp.float32), -6.0, 6.0)
    return drawn.astype(jnp.bfloat16)


def draw_cache_len(key, part):
    key = jax.random.fold_in(key, 5)
    lengths = jax.random.randint(key, (NROWS,), 1, CACHE + 1, dtype=jnp.int32)
    return lengths.at[0].set(CACHE).at[1].set(1)


def levels(rng, extent, cuts, smallest, largest):
    loudness, own = 1.0, jax.random.fold_in(rng, 6)
    for position, blocks in cuts:
        draws = jnp.exp(jax.random.uniform(jax.random.fold_in(own, position), (blocks,), jnp.float32, smallest / len(cuts), largest / len(cuts)))
        loudness = loudness * jnp.repeat(draws, extent[position] // blocks).reshape([-1 if axis == position else 1 for axis in range(len(extent))])
    return loudness


def noise(rng, shape, scale, bound, pieces=(), kind=jnp.bfloat16):
    drawn = scale * jax.random.normal(rng, shape, jnp.float32)
    if pieces:
        drawn = drawn * levels(rng, shape, pieces, -0.22, 0.18)
    return jnp.clip(drawn, -bound, bound).astype(kind)


def setup_inputs(seed: int = 0) -> dict:
    streams_of = jax.random.split(jax.random.key(seed), 10)
    return {
        "prompt_query": draw_prompt_query(jax.random.fold_in(streams_of[9], 71), 0),
        "prompt_keys": draw_prompt_keys(jax.random.fold_in(streams_of[9], 71), 0),
        "prompt_values": noise(streams_of[2], (PROMPT, KV_HEADS, D_HEAD), 1.0, 6.0, ((0, 64), (1, 8))),
        "decode_query": draw_decode_query(jax.random.fold_in(streams_of[9], 71), 0),
        "new_keys": draw_new_keys(jax.random.fold_in(streams_of[9], 71), 0),
        "new_values": noise(streams_of[5], (NROWS, STEPS, KV_HEADS, D_HEAD), 1.0, 6.0, ((0, 512),)),
        "cache_keys": noise(streams_of[6], (NROWS, CACHE, KV_HEADS, D_HEAD), 1.0, 6.0, ((0, 64), (2, 8))),
        "cache_values": noise(streams_of[7], (NROWS, CACHE, KV_HEADS, D_HEAD), 1.0, 6.0, ((0, 64), (2, 8))),
        "cache_len": draw_cache_len(jax.random.fold_in(streams_of[9], 71), 0),
    }


NEG = -1e30


def settle(weights):
    return lax.optimization_barrier(weights.astype(jnp.bfloat16)).astype(jnp.float32)


def prompt_head(query, keys, values):
    total = keys.shape[0]
    width = math.gcd(total, 512)
    scale = query.shape[-1] ** -0.5
    keys_f = keys.astype(jnp.float32)
    values_f = values.astype(jnp.float32)
    positions = jnp.arange(total, dtype=jnp.int32)

    def one_block(index):
        start = (index * width).astype(jnp.int32)
        block = lax.dynamic_slice_in_dim(query, start, width, 0).astype(jnp.float32)
        scores = jnp.einsum("qgd,kd->qgk", block, keys_f) * scale
        row_ids = start + jnp.arange(width, dtype=jnp.int32)
        allowed = (positions[None, :] <= row_ids[:, None])[:, None, :]
        scores = jnp.where(allowed, scores, NEG)
        top = jnp.max(scores, axis=-1, keepdims=True)
        weights = jnp.where(allowed, jnp.exp(scores - top), 0.0)
        totals = jnp.sum(weights, axis=-1)
        mixed = jnp.einsum("qgk,kd->qgd", settle(weights), values_f)
        return (mixed / totals[..., None]).astype(jnp.bfloat16)

    blocks = lax.map(one_block, jnp.arange(total // width, dtype=jnp.int32))
    return blocks.reshape(query.shape)


def reference(prompt_query, prompt_keys, prompt_values, decode_query, new_keys, new_values, cache_keys, cache_values, cache_len):
    heads_out = []
    for head in range(KV_HEADS):
        heads_out.append(prompt_head(prompt_query[:, head], prompt_keys[:, head], prompt_values[:, head]))
    prompt_attn = jnp.stack(heads_out, axis=1)

    scale = D_HEAD ** -0.5
    prefix_kf = prompt_keys.astype(jnp.float32)
    prefix_vf = prompt_values.astype(jnp.float32)
    width = math.gcd(NROWS, 16)
    count = NROWS // width
    slots = jnp.arange(CACHE, dtype=jnp.int32)
    step_ids = jnp.arange(STEPS, dtype=jnp.int32)
    new_ok = (step_ids[None, :] <= step_ids[:, None])[None, :, None, None, :]

    def decode_block(items):
        query, fresh_k, fresh_v, own_k, own_v, lengths = items
        qf = query.astype(jnp.float32)
        s_pre = jnp.einsum("rshgd,khd->rshgk", qf, prefix_kf) * scale
        s_cache = jnp.einsum("rshgd,rchd->rshgc", qf, own_k.astype(jnp.float32)) * scale
        cache_ok = (slots[None, :] < lengths[:, None])[:, None, None, None, :]
        s_cache = jnp.where(cache_ok, s_cache, NEG)
        s_new = jnp.einsum("rshgd,rthd->rshgt", qf, fresh_k.astype(jnp.float32)) * scale
        s_new = jnp.where(new_ok, s_new, NEG)
        top = jnp.maximum(jnp.max(s_pre, axis=-1), jnp.maximum(jnp.max(s_cache, axis=-1), jnp.max(s_new, axis=-1)))
        w_pre = jnp.exp(s_pre - top[..., None])
        w_cache = jnp.where(cache_ok, jnp.exp(s_cache - top[..., None]), 0.0)
        w_new = jnp.where(new_ok, jnp.exp(s_new - top[..., None]), 0.0)
        totals = jnp.sum(w_pre, axis=-1) + jnp.sum(w_cache, axis=-1) + jnp.sum(w_new, axis=-1)
        mixed = jnp.einsum("rshgk,khd->rshgd", settle(w_pre), prefix_vf)
        mixed = mixed + jnp.einsum("rshgc,rchd->rshgd", settle(w_cache), own_v.astype(jnp.float32))
        mixed = mixed + jnp.einsum("rshgt,rthd->rshgd", settle(w_new), fresh_v.astype(jnp.float32))
        return (mixed / totals[..., None]).astype(jnp.bfloat16)

    def split(array):
        return array.reshape((count, width) + array.shape[1:])

    blocks = lax.map(decode_block, (split(decode_query), split(new_keys), split(new_values), split(cache_keys), split(cache_values), split(cache_len)))
    decoded = blocks.reshape(decode_query.shape)
    return prompt_attn, decoded
```

```python
import functools
import math

import jax
import jax.numpy as jnp
from jax import lax
from jax.experimental import pallas as pl
from jax.experimental.pallas import tpu as pltpu
from jax.sharding import PartitionSpec as P

NEG = -1e30
MESH = pl.DeviceIdType.MESH
TILE = 256
ONES = 16


def kernel(
    n, peers, slots, steps, groups, scale2,
    pq_hbm, k_hbm, v_hbm, dq_hbm, nk_hbm, nv_hbm, ck_hbm, cv_hbm, lens_ref,
    out_ref, dec_ref,
    kv, qt, acc, top, inbox, outbox, back, ck, cv,
    pq_ref, k_ref, v_ref, dq, nk, nv, pack_ref, score_a, score_b, high_a, high_b,
    ring_send, ring_recv, sib_send, sib_recv, y_send, y_recv,
    in_send, in_recv, out_send, out_recv, load_sem,
):
    i = lax.axis_index("ctx")
    sec = lax.axis_index("sec")
    tp = lax.axis_index("tp")
    half = n // 2
    h, c = sec // 2, lax.rem(sec, 2)
    right = lax.rem(i + 1, n)
    left = lax.rem(i + n - 1, n)
    to_right, to_left = (right, sec, tp), (left, sec, tp)
    sibling = (i, h * 2 + 1 - c, tp)
    across = (i, (1 - h) * 2 + c, tp)
    width = k_ref.shape[0]
    block = 4 * width
    ptiles = pq_ref.shape[0] // TILE
    dtiles = qt.shape[0] - ptiles
    drows = outbox.shape[1]
    srcs = TILE // drows

    barrier = pltpu.get_barrier_semaphore()
    for device in (to_right, to_left, sibling, across):
        pl.semaphore_signal(barrier, inc=1, device_id=device, device_id_type=MESH)
    for j in range(1, peers):
        device = (i, sec, lax.rem(tp + j, peers))
        pl.semaphore_signal(barrier, inc=1, device_id=device, device_id_type=MESH)

    sources = (k_hbm, v_hbm, dq_hbm, nk_hbm, nv_hbm, pq_hbm, ck_hbm, cv_hbm)
    targets = (k_ref, v_ref, dq, nk, nv, pq_ref, ck, cv)
    loads = [
        pltpu.make_async_copy(source, target, load_sem.at[at])
        for at, (source, target) in enumerate(zip(sources, targets))
    ]
    for load in loads:
        load.start()
    loads[0].wait()
    loads[1].wait()
    kv[i, c, h, 0] = k_ref[...]
    kv[i, c, h, 1] = v_ref[...].astype(jnp.float32).T.astype(jnp.bfloat16)
    for at in range(2, 5):
        loads[at].wait()
    queries = jnp.swapaxes(dq[...].astype(jnp.float32), 0, 1).reshape(peers, drows, -1)
    pack_ref[:, :drows, :] = queries.astype(jnp.bfloat16)
    pack_ref[:, drows:, :] = jnp.concatenate(
        [jnp.swapaxes(new[...].astype(jnp.float32), 0, 1) for new in (nk, nv)], axis=1
    ).astype(jnp.bfloat16)
    pl.semaphore_wait(barrier, 3 + peers)

    def ring(d, s, hh):
        z = lax.rem(i + n - s, n) if d == 0 else lax.rem(i + s, n)
        return pltpu.make_async_remote_copy(
            src_ref=kv.at[z, c, hh],
            dst_ref=kv.at[z, c, hh],
            send_sem=ring_send.at[d, s, hh],
            recv_sem=ring_recv.at[d, s + 1, hh],
            device_id=to_right if d == 0 else to_left,
            device_id_type=MESH,
        )

    def side(d, s, hh, core):
        z = lax.rem(i + n - s, n) if d == 0 else lax.rem(i + s, n)
        return pltpu.make_async_remote_copy(
            src_ref=kv.at[z, core, hh],
            dst_ref=kv.at[z, core, hh],
            send_sem=sib_send.at[d, s, hh],
            recv_sem=sib_recv.at[d, s, hh],
            device_id=sibling,
            device_id_type=MESH,
        )

    def cross(hh):
        return pltpu.make_async_remote_copy(
            src_ref=kv.at[i, c, hh],
            dst_ref=kv.at[i, c, hh],
            send_sem=y_send.at[0],
            recv_sem=y_recv.at[0],
            device_id=across,
            device_id_type=MESH,
        )

    def inward(j):
        to = lax.rem(tp + j, peers)
        return pltpu.make_async_remote_copy(
            src_ref=pack_ref.at[to],
            dst_ref=inbox.at[tp],
            send_sem=in_send.at[j],
            recv_sem=in_recv.at[j],
            device_id=(i, sec, to),
            device_id_type=MESH,
        )

    def inward_wait(j):
        source = lax.rem(tp + peers - j, peers)
        pltpu.make_async_remote_copy(
            src_ref=pack_ref.at[source],
            dst_ref=inbox.at[source],
            send_sem=in_send.at[j],
            recv_sem=in_recv.at[j],
            device_id=(i, sec, source),
            device_id_type=MESH,
        ).wait_recv()

    def outward(j):
        to = lax.rem(tp + j, peers)
        return pltpu.make_async_remote_copy(
            src_ref=outbox.at[to],
            dst_ref=back.at[tp],
            send_sem=out_send.at[j],
            recv_sem=out_recv.at[j],
            device_id=(i, sec, to),
            device_id_type=MESH,
        )

    def outward_wait(j):
        source = lax.rem(tp + peers - j, peers)
        pltpu.make_async_remote_copy(
            src_ref=outbox.at[source],
            dst_ref=back.at[source],
            send_sem=out_send.at[j],
            recv_sem=out_recv.at[j],
            device_id=(i, sec, source),
            device_id_type=MESH,
        ).wait_recv()

    cross(h).start()
    ring(0, 0, h).start()
    ring(1, 0, h).start()
    for j in range(1, peers):
        inward(j).start()
    side(0, 0, h, c).start()
    inbox[tp] = pack_ref[tp]
    loads[5].wait()

    def prepare(t, _):
        rows = pq_ref[pl.ds(pl.multiple_of(t * TILE, TILE), TILE), :]
        qt[t] = rows.astype(jnp.float32).T.astype(jnp.bfloat16)
        return 0

    lax.fori_loop(0, ptiles, prepare, 0)

    cross(1 - h).wait_recv()
    ring(0, 0, 1 - h).start()
    ring(1, 0, 1 - h).start()
    side(0, 0, 1 - h, c).start()

    def keys_of(z):
        return kv[z, :, :, 0].reshape(block, k_ref.shape[1])

    def values_of(z):
        parts = [kv[z, a, b, 1] for a in range(2) for b in range(2)]
        return jnp.concatenate(
            [jnp.concatenate(parts, axis=1), jnp.ones((ONES, block), jnp.bfloat16)], axis=0
        )

    def score(z, t, scores, high, mask=None):
        found = jnp.dot(keys_of(z), qt[t], preferred_element_type=jnp.float32)
        if mask is not None:
            found = jnp.where(mask(t), found, NEG)
        scores[...] = found
        high[...] = jnp.max(found, axis=0, keepdims=True)

    def mix(z, t, scores, high, first=False):
        best = high[...]
        if not first:
            before = top[t]
            best = jnp.maximum(before, best)
        weights = jnp.exp2((scores[...] - best) * scale2).astype(jnp.bfloat16)
        mixed = jnp.dot(values_of(z), weights, preferred_element_type=jnp.float32)
        if not first:
            mixed = acc[t] * jnp.exp2((before - best) * scale2) + mixed
        acc[t] = mixed
        top[t] = best

    def stream(count, item, first=False, mask=None):
        def one(u, _):
            now, second = item(2 * u), item(2 * u + 1)
            later = item(jnp.minimum(2 * u + 2, count - 1))
            score(*second, score_b, high_b, mask)
            mix(*now, score_a, high_a, first)
            score(*later, score_a, high_a, mask)
            mix(*second, score_b, high_b, first)
            return 0

        score(*item(0), score_a, high_a, mask)
        lax.fori_loop(0, count // 2, one, 0)

    def causal(t):
        slot = lax.broadcasted_iota(jnp.int32, (block, TILE), 0)
        core, upper = slot // (2 * width), lax.rem(slot // width, 2)
        position = (upper * 2 + core) * width + lax.rem(slot, width)
        query = (t * TILE + lax.broadcasted_iota(jnp.int32, (block, TILE), 1)) // 2
        return position <= query

    def sweep(z, start, stop):
        stream(stop - start, lambda e: (z, start + e))

    def relay(s):
        for order in range(2):
            hh = h if order == 0 else 1 - h
            for d in range(2):
                ring(d, s - 1, hh).wait_recv()

                @pl.when((s < half - 1) | (hh == d))
                def _():
                    ring(d, s, hh).start()

                side(d, s, hh, c).start()

    relay(jnp.int32(1))
    side(0, 0, 0, 1 - c).wait_recv()
    side(0, 0, 1, 1 - c).wait_recv()
    stream(ptiles, lambda e: (i, e), first=True, mask=causal)

    for j in range(1, peers):
        inward_wait(j)
    for load in loads[6:]:
        load.wait()
    relay(jnp.int32(2))
    for t in range(dtiles):
        rows = inbox[t * srcs : (t + 1) * srcs, :drows, :].reshape(TILE, -1)
        qt[ptiles + t] = rows.astype(jnp.float32).T.astype(jnp.bfloat16)

    per = steps * groups
    own = 128 // per
    pairs = 128 // drows
    fresh = (inbox.shape[1] - drows) // 2

    def private(t, a):
        begin = (t * 2 + a) * own
        queries = qt[ptiles + t, :, a * 128 : (a + 1) * 128]
        keys = ck[begin : begin + own].reshape(own * slots, -1)
        values = cv[begin : begin + own].reshape(own * slots, -1)
        s_cache = jnp.dot(keys, queries, preferred_element_type=jnp.float32)
        slot = lax.broadcasted_iota(jnp.int32, (slots, 128), 0)
        lane_row = lax.broadcasted_iota(jnp.int32, (slots, 128), 1) // per
        allowed = jnp.concatenate(
            [
                (slot < lens_ref[begin + r]) & (lane_row == r)
                for r in range(own)
            ],
            axis=0,
        )
        s_cache = jnp.where(allowed, s_cache, NEG)
        source = (t * 2 + a) * pairs
        new_k = jnp.concatenate(
            [inbox[source + b, drows : drows + 2 * fresh, :] for b in range(pairs)], axis=0
        )
        s_new = jnp.dot(new_k, queries, preferred_element_type=jnp.float32)
        shape = (pairs * 2 * fresh, 128)
        key_id = lax.broadcasted_iota(jnp.int32, shape, 0)
        lane = lax.broadcasted_iota(jnp.int32, shape, 1)
        in_pair = lax.rem(key_id, 2 * fresh)
        key_row = key_id // (2 * fresh) * (fresh // steps) + in_pair // steps
        key_step = lax.rem(in_pair, steps)
        ok = (
            (in_pair < fresh)
            & (key_row == lane // per)
            & (key_step <= lax.rem(lane, per) // groups)
        )
        s_new = jnp.where(ok, s_new, NEG)
        best = jnp.maximum(
            jnp.max(s_cache, axis=0, keepdims=True), jnp.max(s_new, axis=0, keepdims=True)
        )
        w_cache = jnp.exp2((s_cache - best) * scale2)
        w_new = jnp.exp2((s_new - best) * scale2)
        sums = jnp.sum(w_cache, axis=0, keepdims=True) + jnp.sum(w_new, axis=0, keepdims=True)
        new_v = jnp.concatenate(
            [
                jnp.roll(inbox[source + b, drows : drows + 2 * fresh, :].astype(jnp.float32), -fresh, axis=0)
                for b in range(pairs)
            ],
            axis=0,
        ).astype(jnp.bfloat16)
        contract = (((0,), (0,)), ((), ()))
        mixed = lax.dot_general(
            values, w_cache.astype(jnp.bfloat16), contract, preferred_element_type=jnp.float32
        ) + lax.dot_general(
            new_v, w_new.astype(jnp.bfloat16), contract, preferred_element_type=jnp.float32
        )
        depth = mixed.shape[0]
        acc[ptiles + t, :depth, a * 128 : (a + 1) * 128] = mixed
        acc[ptiles + t, depth:, a * 128 : (a + 1) * 128] = jnp.broadcast_to(sums, (ONES, 128))
        top[ptiles + t, :, a * 128 : (a + 1) * 128] = best

    for t in range(dtiles):
        for a in range(2):
            private(t, a)
    sweep(i, ptiles, ptiles + dtiles)

    tiles = ptiles + dtiles

    def work(s):
        z_right, z_left = lax.rem(i + n - s, n), lax.rem(i + s, n)
        for d in range(2):
            side(d, s, 0, 1 - c).wait_recv()
            side(d, s, 1, 1 - c).wait_recv()
        low_right = jnp.where(z_right < i, 0, ptiles)
        low_left = jnp.where(z_left < i, 0, ptiles)
        turn = tiles - low_right

        def item(e):
            rightward = e < turn
            z = jnp.where(rightward, z_right, z_left)
            t = jnp.where(rightward, low_right + e, low_left + e - turn)
            return z, t

        stream(turn + tiles - low_left, item)

    def step(s, _):
        relay(s)
        work(s - 1)
        return 0

    work(jnp.int32(1))
    lax.fori_loop(3, half, step, 0)
    for d in range(2):
        ring(d, half - 1, d).wait_recv()
        side(d, half, d, c).start()
    work(jnp.int32(half - 1))
    for d in range(2):
        side(d, half, d, 1 - c).wait_recv()
    z = lax.rem(i + half, n)
    sweep(z, ptiles, ptiles + dtiles)

    depth = acc.shape[1] - ONES
    for t in range(dtiles):
        total = acc[ptiles + t, depth : depth + 1, :]
        rows = (acc[ptiles + t, :depth, :] / total).T.astype(jnp.bfloat16)
        outbox[t * srcs : (t + 1) * srcs] = rows.reshape(srcs, drows, -1)
    for j in range(1, peers):
        outward(j).start()
    back[tp] = outbox[tp]

    @pl.when(z < i)
    def _():
        sweep(z, 0, ptiles)

    def finish(t, _):
        total = acc[t, depth : depth + 1, :]
        rows = (acc[t, :depth, :] / total).T.astype(jnp.bfloat16)
        out_ref[pl.ds(pl.multiple_of(t * TILE, TILE), TILE), :] = rows
        return 0

    lax.fori_loop(0, ptiles, finish, 0)

    cross(h).wait_send()
    for hh in range(2):
        side(0, 0, hh, c).wait_send()
        for d in range(2):
            ring(d, 0, hh).wait_send()

    def drain(s, _):
        for hh in range(2):
            for d in range(2):
                side(d, s, hh, c).wait_send()

                @pl.when((s < half - 1) | (hh == d))
                def _():
                    ring(d, s, hh).wait_send()

        return 0

    lax.fori_loop(1, half, drain, 0)
    for d in range(2):
        side(d, half, d, c).wait_send()
    for j in range(1, peers):
        inward(j).wait_send()
    for j in range(1, peers):
        outward_wait(j)
    rows = back[...].astype(jnp.float32).reshape(peers, (drows // groups), groups, -1)
    rows = jnp.swapaxes(rows, 0, 1).reshape((drows // groups), peers * groups, -1)
    dec_ref[...] = rows.astype(jnp.bfloat16)
    for j in range(1, peers):
        outward(j).wait_send()


def shards(n, peers, pq, pk, pv, dq, nk, nv, ck, cv, lens):
    rows, _, mine, size = pq.shape
    width = pk.shape[0]
    drow, steps, heads, groups, _ = dq.shape
    own_rows, slots = ck.shape[0], ck.shape[1]
    dr = drow * steps * groups
    fr = drow * steps
    nq = rows * mine
    nd = own_rows * steps * groups
    tiles = (nq + nd) // TILE
    half = n // 2
    bf = jnp.bfloat16
    dma = pltpu.SemaphoreType.DMA
    vmem = pl.BlockSpec(memory_space=pltpu.VMEM)
    hbm = pl.BlockSpec(memory_space=pl.ANY)
    out, dec = pl.pallas_call(
        functools.partial(
            kernel, n, peers, slots, steps, groups, size**-0.5 * math.log2(math.e)
        ),
        out_shape=(
            jax.ShapeDtypeStruct((nq, size), bf),
            jax.ShapeDtypeStruct((fr, heads * groups, size), bf),
        ),
        in_specs=[hbm] * 8 + [pl.BlockSpec(memory_space=pltpu.SMEM)],
        out_specs=(vmem, vmem),
        scratch_shapes=[
            pltpu.VMEM((n, 2, 2, 2, width, size), bf),
            pltpu.VMEM((tiles, size, TILE), bf),
            pltpu.VMEM((tiles, size + ONES, TILE), jnp.float32),
            pltpu.VMEM((tiles, 1, TILE), jnp.float32),
            pltpu.VMEM((peers, dr + 2 * fr, size), bf),
            pltpu.VMEM((peers, dr, size), bf),
            pltpu.VMEM((peers, dr, size), bf),
            pltpu.VMEM((own_rows, slots, size), bf),
            pltpu.VMEM((own_rows, slots, size), bf),
            pltpu.VMEM((nq, size), bf),
            pltpu.VMEM((width, size), bf),
            pltpu.VMEM((width, size), bf),
            pltpu.VMEM((fr, heads, groups, size), bf),
            pltpu.VMEM((fr, heads, size), bf),
            pltpu.VMEM((fr, heads, size), bf),
            pltpu.VMEM((peers, dr + 2 * fr, size), bf),
            pltpu.VMEM((4 * width, TILE), jnp.float32),
            pltpu.VMEM((4 * width, TILE), jnp.float32),
            pltpu.VMEM((1, TILE), jnp.float32),
            pltpu.VMEM((1, TILE), jnp.float32),
            dma((2, half + 1, 2)),
            dma((2, half + 1, 2)),
            dma((2, half + 1, 2)),
            dma((2, half + 1, 2)),
            dma((1,)),
            dma((1,)),
            dma((peers,)),
            dma((peers,)),
            dma((peers,)),
            dma((peers,)),
            dma((8,)),
        ],
        compiler_params=pltpu.CompilerParams(
            collective_id=0, has_side_effects=True, vmem_limit_bytes=60 * 1024 * 1024
        ),
        cost_estimate=pl.CostEstimate(
            flops=4 * (nq + nd) * n * 4 * width * size,
            bytes_accessed=8 * 1024 * 1024,
            transcendentals=(nq + nd) * n * 4 * width,
        ),
        name="shared_prompt_attention",
    )(
        pq.reshape(nq, size),
        pk.reshape(width, size),
        pv.reshape(width, size),
        dq.reshape(fr, heads, groups, size),
        nk.reshape(fr, heads, size),
        nv.reshape(fr, heads, size),
        ck.reshape(own_rows, slots, size),
        cv.reshape(own_rows, slots, size),
        lens,
    )
    return out.reshape(pq.shape), dec.reshape(dq.shape)


def solution(mesh):
    return jax.shard_map(
        functools.partial(shards, mesh.shape["ctx"], mesh.shape["tp"]),
        mesh=mesh,
        in_specs=(
            P("ctx", "tp", "sec", None),
            P(("ctx", "sec"), "tp", None),
            P(("ctx", "sec"), "tp", None),
            P(("ctx", "sec", "tp"), None, None, None, None),
            P(("ctx", "sec", "tp"), None, None, None),
            P(("ctx", "sec", "tp"), None, None, None),
            P(("ctx", "sec"), None, "tp", None),
            P(("ctx", "sec"), None, "tp", None),
            P(("ctx", "sec")),
        ),
        out_specs=(P("ctx", "tp", "sec", None), P(("ctx", "sec", "tp"), None, None, None, None)),
        check_vma=False,
    )
```

```python
import functools
import math

import jax
import jax.numpy as jnp
from jax import lax
from jax.experimental import pallas as pl
from jax.experimental.pallas import tpu as pltpu
from jax.sharding import PartitionSpec as P

NEG = -1e30
MESH = pl.DeviceIdType.MESH
TILE = 512
ONES = 16


def kernel(
    n, peers, slots, steps, groups, scale2,
    pq_hbm, k_hbm, v_hbm, dq_hbm, nk_hbm, nv_hbm, ck_hbm, cv_hbm, lens_ref,
    out_ref, dec_ref,
    kv, qt, acc, top, inbox, outbox, back, ck, cv,
    pq_ref, k_ref, v_ref, dq, nk, nv, pack_ref, score_a, score_b, high_a, high_b,
    ring_send, ring_recv, sib_send, sib_recv, y_send, y_recv,
    in_send, in_recv, out_send, out_recv, load_sem,
):
    i = lax.axis_index("ctx")
    sec = lax.axis_index("sec")
    tp = lax.axis_index("tp")
    half = n // 2
    h, c = sec // 2, lax.rem(sec, 2)
    right = lax.rem(i + 1, n)
    left = lax.rem(i + n - 1, n)
    to_right, to_left = (right, sec, tp), (left, sec, tp)
    sibling = (i, h * 2 + 1 - c, tp)
    across = (i, (1 - h) * 2 + c, tp)
    width = k_ref.shape[0]
    block = 4 * width
    ptiles = pq_ref.shape[0] // TILE
    dtiles = qt.shape[0] - ptiles
    drows = outbox.shape[1]
    srcs = TILE // drows

    barrier = pltpu.get_barrier_semaphore()
    for device in (to_right, to_left, sibling, across):
        pl.semaphore_signal(barrier, inc=1, device_id=device, device_id_type=MESH)
    for j in range(1, peers):
        device = (i, sec, lax.rem(tp + j, peers))
        pl.semaphore_signal(barrier, inc=1, device_id=device, device_id_type=MESH)

    sources = (k_hbm, v_hbm, dq_hbm, nk_hbm, nv_hbm, pq_hbm, ck_hbm, cv_hbm)
    targets = (k_ref, v_ref, dq, nk, nv, pq_ref, ck, cv)
    loads = [
        pltpu.make_async_copy(source, target, load_sem.at[at])
        for at, (source, target) in enumerate(zip(sources, targets))
    ]
    for load in loads:
        load.start()
    loads[0].wait()
    loads[1].wait()
    kv[i, c, h, 0] = k_ref[...]
    kv[i, c, h, 1] = v_ref[...].astype(jnp.float32).T.astype(jnp.bfloat16)
    pl.semaphore_wait(barrier, 3 + peers)

    def ring(d, s, hh):
        z = lax.rem(i + n - s, n) if d == 0 else lax.rem(i + s, n)
        return pltpu.make_async_remote_copy(
            src_ref=kv.at[z, c, hh],
            dst_ref=kv.at[z, c, hh],
            send_sem=ring_send.at[d, s, hh],
            recv_sem=ring_recv.at[d, s + 1, hh],
            device_id=to_right if d == 0 else to_left,
            device_id_type=MESH,
        )

    def side(d, s, hh, core):
        z = lax.rem(i + n - s, n) if d == 0 else lax.rem(i + s, n)
        return pltpu.make_async_remote_copy(
            src_ref=kv.at[z, core, hh],
            dst_ref=kv.at[z, core, hh],
            send_sem=sib_send.at[d, s, hh],
            recv_sem=sib_recv.at[d, s, hh],
            device_id=sibling,
            device_id_type=MESH,
        )

    def cross(hh):
        return pltpu.make_async_remote_copy(
            src_ref=kv.at[i, c, hh],
            dst_ref=kv.at[i, c, hh],
            send_sem=y_send.at[0],
            recv_sem=y_recv.at[0],
            device_id=across,
            device_id_type=MESH,
        )

    def inward(j):
        to = lax.rem(tp + j, peers)
        return pltpu.make_async_remote_copy(
            src_ref=pack_ref.at[to],
            dst_ref=inbox.at[tp],
            send_sem=in_send.at[j],
            recv_sem=in_recv.at[j],
            device_id=(i, sec, to),
            device_id_type=MESH,
        )

    def inward_wait(j):
        source = lax.rem(tp + peers - j, peers)
        pltpu.make_async_remote_copy(
            src_ref=pack_ref.at[source],
            dst_ref=inbox.at[source],
            send_sem=in_send.at[j],
            recv_sem=in_recv.at[j],
            device_id=(i, sec, source),
            device_id_type=MESH,
        ).wait_recv()

    def outward(j):
        to = lax.rem(tp + j, peers)
        return pltpu.make_async_remote_copy(
            src_ref=outbox.at[to],
            dst_ref=back.at[tp],
            send_sem=out_send.at[j],
            recv_sem=out_recv.at[j],
            device_id=(i, sec, to),
            device_id_type=MESH,
        )

    def outward_wait(j):
        source = lax.rem(tp + peers - j, peers)
        pltpu.make_async_remote_copy(
            src_ref=outbox.at[source],
            dst_ref=back.at[source],
            send_sem=out_send.at[j],
            recv_sem=out_recv.at[j],
            device_id=(i, sec, source),
            device_id_type=MESH,
        ).wait_recv()

    cross(h).start()
    ring(0, 0, h).start()
    ring(1, 0, h).start()
    side(0, 0, h, c).start()
    for at in range(2, 5):
        loads[at].wait()
    queries = jnp.swapaxes(dq[...].astype(jnp.float32), 0, 1).reshape(peers, drows, -1)
    pack_ref[:, :drows, :] = queries.astype(jnp.bfloat16)
    pack_ref[:, drows:, :] = jnp.concatenate(
        [jnp.swapaxes(new[...].astype(jnp.float32), 0, 1) for new in (nk, nv)], axis=1
    ).astype(jnp.bfloat16)
    for j in range(1, peers):
        inward(j).start()
    inbox[tp] = pack_ref[tp]
    loads[5].wait()

    def prepare(t, _):
        rows = pq_ref[pl.ds(pl.multiple_of(t * TILE, TILE), TILE), :]
        qt[t] = rows.astype(jnp.float32).T.astype(jnp.bfloat16)
        return 0

    lax.fori_loop(0, ptiles, prepare, 0)

    cross(1 - h).wait_recv()
    ring(0, 0, 1 - h).start()
    ring(1, 0, 1 - h).start()
    side(0, 0, 1 - h, c).start()

    parts = 2
    span = block // parts

    def advance(now, later, scores, high, scores_next, high_next, first, mask):
        z, t = now
        best = high[...]
        if not first:
            before = top[t]
            best = jnp.maximum(before, best)
        peak, weights = None, []
        for part in range(parts):
            rows = slice(part * span, (part + 1) * span)
            if later is not None:
                found = ahead(*later, part, mask)
                scores_next[rows] = found
                part_peak = jnp.max(found, axis=0, keepdims=True)
                peak = part_peak if peak is None else jnp.maximum(peak, part_peak)
            weights.append(jnp.exp2((scores[rows] - best) * scale2).astype(jnp.bfloat16))
        values = jnp.concatenate([kv[z, a, b, 1] for a in range(2) for b in range(2)], axis=1)
        values = jnp.concatenate([values, jnp.ones((ONES, block), jnp.bfloat16)], axis=0)
        mixed = jnp.dot(
            values, jnp.concatenate(weights, axis=0), preferred_element_type=jnp.float32
        )
        if later is not None:
            high_next[...] = peak
        if not first:
            mixed = acc[t] * jnp.exp2((before - best) * scale2) + mixed
        acc[t] = mixed
        top[t] = best

    def ahead(z, t, part, mask):
        keys = kv[z, part, :, 0].reshape(span, k_ref.shape[1])
        found = jnp.dot(keys, qt[t], preferred_element_type=jnp.float32)
        return found if mask is None else jnp.where(mask(t, part), found, NEG)

    def begin(z, t, mask=None):
        peak = None
        for part in range(parts):
            found = ahead(z, t, part, mask)
            score_a[part * span : (part + 1) * span] = found
            part_peak = jnp.max(found, axis=0, keepdims=True)
            peak = part_peak if peak is None else jnp.maximum(peak, part_peak)
        high_a[...] = peak

    def lone(z, t, first=False):
        begin(z, t)
        advance((z, t), None, score_a, high_a, None, None, first, None)

    def stream(count, item, first=False, mask=None, hook=None):
        def one(u, _):
            now, second = item(2 * u), item(2 * u + 1)
            later = item(jnp.minimum(2 * u + 2, count - 1))
            if hook is not None:
                pl.when(u == count // 4)(hook)
            advance(now, second, score_a, high_a, score_b, high_b, first, mask)
            advance(second, later, score_b, high_b, score_a, high_a, first, mask)
            return 0

        begin(*item(0), mask)
        lax.fori_loop(0, count // 2, one, 0)

    def causal(t, part):
        slot = lax.broadcasted_iota(jnp.int32, (span, TILE), 0)
        position = (slot // width * 2 + part) * width + lax.rem(slot, width)
        query = (t * TILE + lax.broadcasted_iota(jnp.int32, (span, TILE), 1)) // 2
        return position <= query

    def relay(s, order):
        hh = h if order == 0 else 1 - h
        for d in range(2):
            ring(d, s - 1, hh).wait_recv()

            @pl.when((s < half - 1) | (hh == d))
            def _():
                ring(d, s, hh).start()

            side(d, s, hh, c).start()

    relay(jnp.int32(1), 0)
    side(0, 0, 0, 1 - c).wait_recv()
    side(0, 0, 1, 1 - c).wait_recv()
    stream(
        jnp.int32(ptiles), lambda e: (i, e), first=True, mask=causal,
        hook=lambda: relay(jnp.int32(1), 1),
    )

    for j in range(1, peers):
        inward_wait(j)
    for t in range(dtiles):
        rows = inbox[t * srcs : (t + 1) * srcs, :drows, :].reshape(TILE, -1)
        qt[ptiles + t] = rows.astype(jnp.float32).T.astype(jnp.bfloat16)

    per = steps * groups
    own = 128 // per
    pairs = 128 // drows
    fresh = (inbox.shape[1] - drows) // 2

    def private(group):
        t, lanes = ptiles + group * 128 // TILE, pl.ds(group * 128 % TILE, 128)
        start = group * own
        queries = qt[t, :, lanes]
        lane_row = lax.broadcasted_iota(jnp.int32, (slots, 128), 1) // per
        limit = jnp.full((slots, 128), lens_ref[start], jnp.int32)
        s_cache = jnp.dot(ck[start], queries, preferred_element_type=jnp.float32)
        for r in range(1, own):
            found = jnp.dot(ck[start + r], queries, preferred_element_type=jnp.float32)
            s_cache = jnp.where(lane_row == r, found, s_cache)
            limit = jnp.where(lane_row == r, lens_ref[start + r], limit)
        slot = lax.broadcasted_iota(jnp.int32, (slots, 128), 0)
        s_cache = jnp.where(slot < limit, s_cache, NEG)
        source = group * pairs
        new_k = jnp.concatenate(
            [inbox[source + b, drows : drows + 2 * fresh, :] for b in range(pairs)], axis=0
        )
        s_new = jnp.dot(new_k, queries, preferred_element_type=jnp.float32)
        shape = (pairs * 2 * fresh, 128)
        key_id = lax.broadcasted_iota(jnp.int32, shape, 0)
        lane = lax.broadcasted_iota(jnp.int32, shape, 1)
        in_pair = lax.rem(key_id, 2 * fresh)
        key_row = key_id // (2 * fresh) * (fresh // steps) + in_pair // steps
        key_step = lax.rem(in_pair, steps)
        ok = (
            (in_pair < fresh)
            & (key_row == lane // per)
            & (key_step <= lax.rem(lane, per) // groups)
        )
        s_new = jnp.where(ok, s_new, NEG)
        before = top[t, :, lanes]
        best = jnp.maximum(
            jnp.max(s_cache, axis=0, keepdims=True), jnp.max(s_new, axis=0, keepdims=True)
        )
        best = jnp.maximum(before, best)
        w_cache = jnp.exp2((s_cache - best) * scale2)
        w_new = jnp.exp2((s_new - best) * scale2)
        sums = jnp.sum(w_cache, axis=0, keepdims=True) + jnp.sum(w_new, axis=0, keepdims=True)
        new_v = jnp.concatenate(
            [
                jnp.roll(
                    inbox[source + b, drows : drows + 2 * fresh, :].astype(jnp.float32),
                    -fresh,
                    axis=0,
                )
                for b in range(pairs)
            ],
            axis=0,
        ).astype(jnp.bfloat16)
        turned = w_cache.T.astype(jnp.bfloat16)
        mixed = jnp.concatenate(
            [
                jnp.dot(
                    turned[r * per : (r + 1) * per],
                    cv[start + r],
                    preferred_element_type=jnp.float32,
                )
                for r in range(own)
            ],
            axis=0,
        ).T + lax.dot_general(
            new_v,
            w_new.astype(jnp.bfloat16),
            (((0,), (0,)), ((), ())),
            preferred_element_type=jnp.float32,
        )
        mixed = jnp.concatenate([mixed, jnp.broadcast_to(sums, (ONES, 128))], axis=0)
        acc[t, :, lanes] = acc[t, :, lanes] * jnp.exp2((before - best) * scale2) + mixed
        top[t, :, lanes] = best

    for t in range(dtiles):
        lone(i, ptiles + t, first=True)
    tiles = ptiles + dtiles

    def work(s, hook=None):
        z_right, z_left = lax.rem(i + n - s, n), lax.rem(i + s, n)
        for d in range(2):
            side(d, s, 0, 1 - c).wait_recv()
            side(d, s, 1, 1 - c).wait_recv()
        low_right = jnp.where(z_right < i, 0, ptiles)
        low_left = jnp.where(z_left < i, 0, ptiles)
        turn = tiles - low_right

        def item(e):
            rightward = e < turn
            z = jnp.where(rightward, z_right, z_left)
            t = jnp.where(rightward, low_right + e, low_left + e - turn)
            return z, t

        stream(turn + tiles - low_left, item, hook=hook)

    relay(jnp.int32(2), 0)
    work(jnp.int32(1), lambda: relay(jnp.int32(2), 1))
    for load in loads[6:]:
        load.wait()
    private_groups = dtiles * TILE // 128

    def step(s, _):
        relay(s, 0)
        for group in range(private_groups):
            pl.when(s == 3 + group)(functools.partial(private, group))
        work(s - 1, lambda: relay(s, 1))
        return 0

    lax.fori_loop(3, half, step, 0)
    for d in range(2):
        ring(d, half - 1, d).wait_recv()
        side(d, half, d, c).start()
    work(jnp.int32(half - 1))
    for d in range(2):
        side(d, half, d, 1 - c).wait_recv()
    z = lax.rem(i + half, n)
    for t in range(dtiles):
        lone(z, ptiles + t)

    depth = acc.shape[1] - ONES
    for t in range(dtiles):
        total = acc[ptiles + t, depth : depth + 1, :]
        rows = (acc[ptiles + t, :depth, :] / total).T.astype(jnp.bfloat16)
        outbox[t * srcs : (t + 1) * srcs] = rows.reshape(srcs, drows, -1)
    for j in range(1, peers):
        outward(j).start()
    back[tp] = outbox[tp]

    @pl.when(z < i)
    def _():
        stream(jnp.int32(ptiles), lambda e: (z, e))

    def finish(t, _):
        total = acc[t, depth : depth + 1, :]
        rows = (acc[t, :depth, :] / total).T.astype(jnp.bfloat16)
        out_ref[pl.ds(pl.multiple_of(t * TILE, TILE), TILE), :] = rows
        return 0

    lax.fori_loop(0, ptiles, finish, 0)

    cross(h).wait_send()
    for hh in range(2):
        side(0, 0, hh, c).wait_send()
        for d in range(2):
            ring(d, 0, hh).wait_send()

    def drain(s, _):
        for hh in range(2):
            for d in range(2):
                side(d, s, hh, c).wait_send()

                @pl.when((s < half - 1) | (hh == d))
                def _():
                    ring(d, s, hh).wait_send()

        return 0

    lax.fori_loop(1, half, drain, 0)
    for d in range(2):
        side(d, half, d, c).wait_send()
    for j in range(1, peers):
        inward(j).wait_send()
    for j in range(1, peers):
        outward_wait(j)
    rows = back[...].astype(jnp.float32).reshape(peers, (drows // groups), groups, -1)
    rows = jnp.swapaxes(rows, 0, 1).reshape((drows // groups), peers * groups, -1)
    dec_ref[...] = rows.astype(jnp.bfloat16)
    for j in range(1, peers):
        outward(j).wait_send()


def shards(n, peers, pq, pk, pv, dq, nk, nv, ck, cv, lens):
    rows, _, mine, size = pq.shape
    width = pk.shape[0]
    drow, steps, heads, groups, _ = dq.shape
    own_rows, slots = ck.shape[0], ck.shape[1]
    dr = drow * steps * groups
    fr = drow * steps
    nq = rows * mine
    nd = own_rows * steps * groups
    tiles = (nq + nd) // TILE
    half = n // 2
    bf = jnp.bfloat16
    dma = pltpu.SemaphoreType.DMA
    vmem = pl.BlockSpec(memory_space=pltpu.VMEM)
    hbm = pl.BlockSpec(memory_space=pl.ANY)
    out, dec = pl.pallas_call(
        functools.partial(
            kernel, n, peers, slots, steps, groups, size**-0.5 * math.log2(math.e)
        ),
        out_shape=(
            jax.ShapeDtypeStruct((nq, size), bf),
            jax.ShapeDtypeStruct((fr, heads * groups, size), bf),
        ),
        in_specs=[hbm] * 8 + [pl.BlockSpec(memory_space=pltpu.SMEM)],
        out_specs=(vmem, vmem),
        scratch_shapes=[
            pltpu.VMEM((n, 2, 2, 2, width, size), bf),
            pltpu.VMEM((tiles, size, TILE), bf),
            pltpu.VMEM((tiles, size + ONES, TILE), jnp.float32),
            pltpu.VMEM((tiles, 1, TILE), jnp.float32),
            pltpu.VMEM((peers, dr + 2 * fr, size), bf),
            pltpu.VMEM((peers, dr, size), bf),
            pltpu.VMEM((peers, dr, size), bf),
            pltpu.VMEM((own_rows, slots, size), bf),
            pltpu.VMEM((own_rows, slots, size), bf),
            pltpu.VMEM((nq, size), bf),
            pltpu.VMEM((width, size), bf),
            pltpu.VMEM((width, size), bf),
            pltpu.VMEM((fr, heads, groups, size), bf),
            pltpu.VMEM((fr, heads, size), bf),
            pltpu.VMEM((fr, heads, size), bf),
            pltpu.VMEM((peers, dr + 2 * fr, size), bf),
            pltpu.VMEM((4 * width, TILE), jnp.float32),
            pltpu.VMEM((4 * width, TILE), jnp.float32),
            pltpu.VMEM((1, TILE), jnp.float32),
            pltpu.VMEM((1, TILE), jnp.float32),
            dma((2, half + 1, 2)),
            dma((2, half + 1, 2)),
            dma((2, half + 1, 2)),
            dma((2, half + 1, 2)),
            dma((1,)),
            dma((1,)),
            dma((peers,)),
            dma((peers,)),
            dma((peers,)),
            dma((peers,)),
            dma((8,)),
        ],
        compiler_params=pltpu.CompilerParams(
            collective_id=0, has_side_effects=True, vmem_limit_bytes=60 * 1024 * 1024
        ),
        cost_estimate=pl.CostEstimate(
            flops=4 * (nq + nd) * n * 4 * width * size,
            bytes_accessed=8 * 1024 * 1024,
            transcendentals=(nq + nd) * n * 4 * width,
        ),
        name="shared_prompt_attention",
    )(
        pq.reshape(nq, size),
        pk.reshape(width, size),
        pv.reshape(width, size),
        dq.reshape(fr, heads, groups, size),
        nk.reshape(fr, heads, size),
        nv.reshape(fr, heads, size),
        ck.reshape(own_rows, slots, size),
        cv.reshape(own_rows, slots, size),
        lens,
    )
    return out.reshape(pq.shape), dec.reshape(dq.shape)


def solution(mesh):
    return jax.shard_map(
        functools.partial(shards, mesh.shape["ctx"], mesh.shape["tp"]),
        mesh=mesh,
        in_specs=(
            P("ctx", "tp", "sec", None),
            P(("ctx", "sec"), "tp", None),
            P(("ctx", "sec"), "tp", None),
            P(("ctx", "sec", "tp"), None, None, None, None),
            P(("ctx", "sec", "tp"), None, None, None),
            P(("ctx", "sec", "tp"), None, None, None),
            P(("ctx", "sec"), None, "tp", None),
            P(("ctx", "sec"), None, "tp", None),
            P(("ctx", "sec")),
        ),
        out_specs=(P("ctx", "tp", "sec", None), P(("ctx", "sec", "tp"), None, None, None, None)),
        check_vma=False,
    )
```

```python
import functools
import math

import jax
import jax.numpy as jnp
from jax import lax
from jax.experimental import pallas as pl
from jax.experimental.pallas import tpu as pltpu
from jax.sharding import PartitionSpec as P

NEG = -1e30
MESH = pl.DeviceIdType.MESH
TILE = 512
ONES = 16


def kernel(
    n, peers, slots, steps, groups, scale2,
    pq_hbm, k_hbm, v_hbm, dq_hbm, nk_hbm, nv_hbm, ck_hbm, cv_hbm, lens_ref,
    out_ref, dec_ref,
    kv, qt, acc, top, inbox, outbox, back, ck, cv,
    pq_ref, k_ref, v_ref, dq, nk, nv, pack_ref, score_a, score_b, high_a, high_b,
    ring_send, ring_recv, sib_send, sib_recv, y_send, y_recv,
    in_send, in_recv, out_send, out_recv, load_sem,
):
    i = lax.axis_index("ctx")
    sec = lax.axis_index("sec")
    tp = lax.axis_index("tp")
    half = n // 2
    h, c = sec // 2, lax.rem(sec, 2)
    right = lax.rem(i + 1, n)
    left = lax.rem(i + n - 1, n)
    to_right, to_left = (right, sec, tp), (left, sec, tp)
    sibling = (i, h * 2 + 1 - c, tp)
    across = (i, (1 - h) * 2 + c, tp)
    width = k_ref.shape[0]
    block = 4 * width
    ptiles = pq_ref.shape[0] // TILE
    dtiles = qt.shape[0] - ptiles
    drows = outbox.shape[1]
    srcs = TILE // drows

    barrier = pltpu.get_barrier_semaphore()
    for device in (to_right, to_left, sibling, across):
        pl.semaphore_signal(barrier, inc=1, device_id=device, device_id_type=MESH)
    for j in range(1, peers):
        device = (i, sec, lax.rem(tp + j, peers))
        pl.semaphore_signal(barrier, inc=1, device_id=device, device_id_type=MESH)

    sources = (k_hbm, v_hbm, dq_hbm, nk_hbm, nv_hbm, pq_hbm, ck_hbm, cv_hbm)
    targets = (k_ref, v_ref, dq, nk, nv, pq_ref, ck, cv)
    loads = [
        pltpu.make_async_copy(source, target, load_sem.at[at])
        for at, (source, target) in enumerate(zip(sources, targets))
    ]
    for load in loads:
        load.start()
    loads[0].wait()
    loads[1].wait()
    kv[i, c, h, 0] = k_ref[...]
    kv[i, c, h, 1] = v_ref[...].astype(jnp.float32).T.astype(jnp.bfloat16)
    pl.semaphore_wait(barrier, 3 + peers)

    def ring(d, s, hh):
        z = lax.rem(i + n - s, n) if d == 0 else lax.rem(i + s, n)
        return pltpu.make_async_remote_copy(
            src_ref=kv.at[z, c, hh],
            dst_ref=kv.at[z, c, hh],
            send_sem=ring_send.at[d, s, hh],
            recv_sem=ring_recv.at[d, s + 1, hh],
            device_id=to_right if d == 0 else to_left,
            device_id_type=MESH,
        )

    def side(d, s, hh, core):
        z = lax.rem(i + n - s, n) if d == 0 else lax.rem(i + s, n)
        return pltpu.make_async_remote_copy(
            src_ref=kv.at[z, core, hh],
            dst_ref=kv.at[z, core, hh],
            send_sem=sib_send.at[d, s, hh],
            recv_sem=sib_recv.at[d, s, hh],
            device_id=sibling,
            device_id_type=MESH,
        )

    def cross(hh):
        return pltpu.make_async_remote_copy(
            src_ref=kv.at[i, c, hh],
            dst_ref=kv.at[i, c, hh],
            send_sem=y_send.at[0],
            recv_sem=y_recv.at[0],
            device_id=across,
            device_id_type=MESH,
        )

    def inward(j):
        to = lax.rem(tp + j, peers)
        return pltpu.make_async_remote_copy(
            src_ref=pack_ref.at[to],
            dst_ref=inbox.at[tp],
            send_sem=in_send.at[j],
            recv_sem=in_recv.at[j],
            device_id=(i, sec, to),
            device_id_type=MESH,
        )

    def inward_wait(j):
        source = lax.rem(tp + peers - j, peers)
        pltpu.make_async_remote_copy(
            src_ref=pack_ref.at[source],
            dst_ref=inbox.at[source],
            send_sem=in_send.at[j],
            recv_sem=in_recv.at[j],
            device_id=(i, sec, source),
            device_id_type=MESH,
        ).wait_recv()

    def outward(j):
        to = lax.rem(tp + j, peers)
        return pltpu.make_async_remote_copy(
            src_ref=outbox.at[to],
            dst_ref=back.at[tp],
            send_sem=out_send.at[j],
            recv_sem=out_recv.at[j],
            device_id=(i, sec, to),
            device_id_type=MESH,
        )

    def outward_wait(j):
        source = lax.rem(tp + peers - j, peers)
        pltpu.make_async_remote_copy(
            src_ref=outbox.at[source],
            dst_ref=back.at[source],
            send_sem=out_send.at[j],
            recv_sem=out_recv.at[j],
            device_id=(i, sec, source),
            device_id_type=MESH,
        ).wait_recv()

    cross(h).start()
    ring(0, 0, h).start()
    ring(1, 0, h).start()
    side(0, 0, h, c).start()
    for at in range(2, 5):
        loads[at].wait()
    queries = jnp.swapaxes(dq[...].astype(jnp.float32), 0, 1).reshape(peers, drows, -1)
    pack_ref[:, :drows, :] = queries.astype(jnp.bfloat16)
    pack_ref[:, drows:, :] = jnp.concatenate(
        [jnp.swapaxes(new[...].astype(jnp.float32), 0, 1) for new in (nk, nv)], axis=1
    ).astype(jnp.bfloat16)
    for j in range(1, peers):
        inward(j).start()
    inbox[tp] = pack_ref[tp]

    def scaled(rows):
        turned = rows.astype(jnp.float32).T * scale2
        high = turned.astype(jnp.bfloat16)
        low = (turned - high.astype(jnp.float32)).astype(jnp.bfloat16)
        return jnp.concatenate([high, low], axis=0)

    def twice(keys):
        return jnp.concatenate([keys, keys], axis=1)

    def prepare(t, _):
        qt[t] = scaled(pq_ref[pl.ds(pl.multiple_of(t * TILE, TILE), TILE), :])
        return 0

    cross(1 - h).wait_recv()
    ring(0, 0, 1 - h).start()
    ring(1, 0, 1 - h).start()
    side(0, 0, 1 - h, c).start()
    loads[5].wait()
    lax.fori_loop(0, ptiles, prepare, 0)

    parts = 2
    span = block // parts

    def advance(now, later, scores, high, scores_next, high_next, first, mask):
        z, t = now
        best = high[...]
        if not first:
            before = top[t]
            best = jnp.maximum(before, best)
        peak, weights = None, []
        for part in range(parts):
            rows = slice(part * span, (part + 1) * span)
            if later is not None:
                found = ahead(*later, part, mask)
                scores_next[rows] = found
                part_peak = jnp.max(found, axis=0, keepdims=True)
                peak = part_peak if peak is None else jnp.maximum(peak, part_peak)
            weights.append(jnp.exp2(scores[rows] - best).astype(jnp.bfloat16))
        values = jnp.concatenate([kv[z, a, b, 1] for a in range(2) for b in range(2)], axis=1)
        values = jnp.concatenate([values, jnp.ones((ONES, block), jnp.bfloat16)], axis=0)
        mixed = jnp.dot(
            values, jnp.concatenate(weights, axis=0), preferred_element_type=jnp.float32
        )
        if later is not None:
            high_next[...] = peak
        if not first:
            mixed = acc[t] * jnp.exp2(before - best) + mixed
        acc[t] = mixed
        top[t] = best

    def ahead(z, t, part, mask):
        keys = kv[z, part, :, 0].reshape(span, k_ref.shape[1])
        found = jnp.dot(twice(keys), qt[t], preferred_element_type=jnp.float32)
        return found if mask is None else jnp.where(mask(t, part), found, NEG)

    def begin(z, t, mask=None):
        peak = None
        for part in range(parts):
            found = ahead(z, t, part, mask)
            score_a[part * span : (part + 1) * span] = found
            part_peak = jnp.max(found, axis=0, keepdims=True)
            peak = part_peak if peak is None else jnp.maximum(peak, part_peak)
        high_a[...] = peak

    def lone(z, t, first=False):
        begin(z, t)
        advance((z, t), None, score_a, high_a, None, None, first, None)

    def stream(count, item, first=False, mask=None, hook=None):
        def one(u, _):
            now, second = item(2 * u), item(2 * u + 1)
            later = item(jnp.minimum(2 * u + 2, count - 1))
            if hook is not None:
                pl.when(u == count // 4)(hook)
            advance(now, second, score_a, high_a, score_b, high_b, first, mask)
            advance(second, later, score_b, high_b, score_a, high_a, first, mask)
            return 0

        begin(*item(0), mask)
        lax.fori_loop(0, count // 2, one, 0)

    def causal(t, part):
        slot = lax.broadcasted_iota(jnp.int32, (span, TILE), 0)
        position = (slot // width * 2 + part) * width + lax.rem(slot, width)
        query = (t * TILE + lax.broadcasted_iota(jnp.int32, (span, TILE), 1)) // 2
        return position <= query

    def relay(s, order):
        hh = h if order == 0 else 1 - h
        for d in range(2):
            ring(d, s - 1, hh).wait_recv()

            @pl.when((s < half - 1) | (hh == d))
            def _():
                ring(d, s, hh).start()

            side(d, s, hh, c).start()

    relay(jnp.int32(1), 0)
    side(0, 0, 0, 1 - c).wait_recv()
    side(0, 0, 1, 1 - c).wait_recv()
    stream(
        jnp.int32(ptiles), lambda e: (i, e), first=True, mask=causal,
        hook=lambda: relay(jnp.int32(1), 1),
    )

    for j in range(1, peers):
        inward_wait(j)
    for t in range(dtiles):
        rows = inbox[t * srcs : (t + 1) * srcs, :drows, :].reshape(TILE, -1)
        qt[ptiles + t] = scaled(rows)

    per = steps * groups
    own = 128 // per
    pairs = 128 // drows
    fresh = (inbox.shape[1] - drows) // 2

    def private(group):
        t, lanes = ptiles + group * 128 // TILE, pl.ds(group * 128 % TILE, 128)
        start = group * own
        queries = qt[t, :, lanes]
        lane_row = lax.broadcasted_iota(jnp.int32, (slots, 128), 1) // per
        limit = jnp.full((slots, 128), lens_ref[start], jnp.int32)
        s_cache = jnp.dot(twice(ck[start]), queries, preferred_element_type=jnp.float32)
        for r in range(1, own):
            found = jnp.dot(twice(ck[start + r]), queries, preferred_element_type=jnp.float32)
            s_cache = jnp.where(lane_row == r, found, s_cache)
            limit = jnp.where(lane_row == r, lens_ref[start + r], limit)
        slot = lax.broadcasted_iota(jnp.int32, (slots, 128), 0)
        s_cache = jnp.where(slot < limit, s_cache, NEG)
        source = group * pairs
        new_k = jnp.concatenate(
            [inbox[source + b, drows : drows + 2 * fresh, :] for b in range(pairs)], axis=0
        )
        s_new = jnp.dot(twice(new_k), queries, preferred_element_type=jnp.float32)
        shape = (pairs * 2 * fresh, 128)
        key_id = lax.broadcasted_iota(jnp.int32, shape, 0)
        lane = lax.broadcasted_iota(jnp.int32, shape, 1)
        in_pair = lax.rem(key_id, 2 * fresh)
        key_row = key_id // (2 * fresh) * (fresh // steps) + in_pair // steps
        key_step = lax.rem(in_pair, steps)
        ok = (
            (in_pair < fresh)
            & (key_row == lane // per)
            & (key_step <= lax.rem(lane, per) // groups)
        )
        s_new = jnp.where(ok, s_new, NEG)
        before = top[t, :, lanes]
        best = jnp.maximum(
            jnp.max(s_cache, axis=0, keepdims=True), jnp.max(s_new, axis=0, keepdims=True)
        )
        best = jnp.maximum(before, best)
        w_cache = jnp.exp2(s_cache - best)
        w_new = jnp.exp2(s_new - best)
        sums = jnp.sum(w_cache, axis=0, keepdims=True) + jnp.sum(w_new, axis=0, keepdims=True)
        new_v = jnp.concatenate(
            [
                jnp.roll(
                    inbox[source + b, drows : drows + 2 * fresh, :].astype(jnp.float32),
                    -fresh,
                    axis=0,
                )
                for b in range(pairs)
            ],
            axis=0,
        ).astype(jnp.bfloat16)
        turned = w_cache.T.astype(jnp.bfloat16)
        mixed = jnp.concatenate(
            [
                jnp.dot(
                    turned[r * per : (r + 1) * per],
                    cv[start + r],
                    preferred_element_type=jnp.float32,
                )
                for r in range(own)
            ],
            axis=0,
        ).T + lax.dot_general(
            new_v,
            w_new.astype(jnp.bfloat16),
            (((0,), (0,)), ((), ())),
            preferred_element_type=jnp.float32,
        )
        mixed = jnp.concatenate([mixed, jnp.broadcast_to(sums, (ONES, 128))], axis=0)
        acc[t, :, lanes] = acc[t, :, lanes] * jnp.exp2(before - best) + mixed
        top[t, :, lanes] = best

    for t in range(dtiles):
        lone(i, ptiles + t, first=True)
    tiles = ptiles + dtiles

    def work(s, hook=None):
        z_right, z_left = lax.rem(i + n - s, n), lax.rem(i + s, n)
        for d in range(2):
            side(d, s, 0, 1 - c).wait_recv()
            side(d, s, 1, 1 - c).wait_recv()
        low_right = jnp.where(z_right < i, 0, ptiles)
        low_left = jnp.where(z_left < i, 0, ptiles)
        turn = tiles - low_right

        def item(e):
            rightward = e < turn
            z = jnp.where(rightward, z_right, z_left)
            t = jnp.where(rightward, low_right + e, low_left + e - turn)
            return z, t

        stream(turn + tiles - low_left, item, hook=hook)

    relay(jnp.int32(2), 0)
    work(jnp.int32(1), lambda: relay(jnp.int32(2), 1))
    for load in loads[6:]:
        load.wait()
    private_groups = dtiles * TILE // 128

    def step(s, _):
        relay(s, 0)
        for group in range(private_groups):
            pl.when(s == 3 + group)(functools.partial(private, group))
        work(s - 1, lambda: relay(s, 1))
        return 0

    lax.fori_loop(3, half, step, 0)

    work(jnp.int32(half - 1))
    for d in range(2):
        ring(d, half - 1, d).wait_recv()
        side(d, half, d, c).start()
    for d in range(2):
        side(d, half, d, 1 - c).wait_recv()
    z = lax.rem(i + half, n)
    for t in range(dtiles):
        lone(z, ptiles + t)

    depth = acc.shape[1] - ONES
    for t in range(dtiles):
        total = acc[ptiles + t, depth : depth + 1, :]
        rows = (acc[ptiles + t, :depth, :] / total).T.astype(jnp.bfloat16)
        outbox[t * srcs : (t + 1) * srcs] = rows.reshape(srcs, drows, -1)
    for j in range(1, peers):
        outward(j).start()
    back[tp] = outbox[tp]

    @pl.when(z < i)
    def _():
        stream(jnp.int32(ptiles), lambda e: (z, e))

    def finish(t, _):
        total = acc[t, depth : depth + 1, :]
        rows = (acc[t, :depth, :] / total).T.astype(jnp.bfloat16)
        out_ref[pl.ds(pl.multiple_of(t * TILE, TILE), TILE), :] = rows
        return 0

    lax.fori_loop(0, ptiles, finish, 0)

    cross(h).wait_send()
    for hh in range(2):
        side(0, 0, hh, c).wait_send()
        for d in range(2):
            ring(d, 0, hh).wait_send()

    def drain(s, _):
        for hh in range(2):
            for d in range(2):
                side(d, s, hh, c).wait_send()

                @pl.when((s < half - 1) | (hh == d))
                def _():
                    ring(d, s, hh).wait_send()

        return 0

    lax.fori_loop(1, half, drain, 0)
    for d in range(2):
        side(d, half, d, c).wait_send()
    for j in range(1, peers):
        inward(j).wait_send()
    for j in range(1, peers):
        outward_wait(j)
    rows = back[...].astype(jnp.float32).reshape(peers, (drows // groups), groups, -1)
    rows = jnp.swapaxes(rows, 0, 1).reshape((drows // groups), peers * groups, -1)
    dec_ref[...] = rows.astype(jnp.bfloat16)
    for j in range(1, peers):
        outward(j).wait_send()


def shards(n, peers, pq, pk, pv, dq, nk, nv, ck, cv, lens):
    rows, _, mine, size = pq.shape
    width = pk.shape[0]
    drow, steps, heads, groups, _ = dq.shape
    own_rows, slots = ck.shape[0], ck.shape[1]
    dr = drow * steps * groups
    fr = drow * steps
    nq = rows * mine
    nd = own_rows * steps * groups
    tiles = (nq + nd) // TILE
    half = n // 2
    bf = jnp.bfloat16
    dma = pltpu.SemaphoreType.DMA
    vmem = pl.BlockSpec(memory_space=pltpu.VMEM)
    hbm = pl.BlockSpec(memory_space=pl.ANY)
    out, dec = pl.pallas_call(
        functools.partial(
            kernel, n, peers, slots, steps, groups, size**-0.5 * math.log2(math.e)
        ),
        out_shape=(
            jax.ShapeDtypeStruct((nq, size), bf),
            jax.ShapeDtypeStruct((fr, heads * groups, size), bf),
        ),
        in_specs=[hbm] * 8 + [pl.BlockSpec(memory_space=pltpu.SMEM)],
        out_specs=(vmem, vmem),
        scratch_shapes=[
            pltpu.VMEM((n, 2, 2, 2, width, size), bf),
            pltpu.VMEM((tiles, 2 * size, TILE), bf),
            pltpu.VMEM((tiles, size + ONES, TILE), jnp.float32),
            pltpu.VMEM((tiles, 1, TILE), jnp.float32),
            pltpu.VMEM((peers, dr + 2 * fr, size), bf),
            pltpu.VMEM((peers, dr, size), bf),
            pltpu.VMEM((peers, dr, size), bf),
            pltpu.VMEM((own_rows, slots, size), bf),
            pltpu.VMEM((own_rows, slots, size), bf),
            pltpu.VMEM((nq, size), bf),
            pltpu.VMEM((width, size), bf),
            pltpu.VMEM((width, size), bf),
            pltpu.VMEM((fr, heads, groups, size), bf),
            pltpu.VMEM((fr, heads, size), bf),
            pltpu.VMEM((fr, heads, size), bf),
            pltpu.VMEM((peers, dr + 2 * fr, size), bf),
            pltpu.VMEM((4 * width, TILE), jnp.float32),
            pltpu.VMEM((4 * width, TILE), jnp.float32),
            pltpu.VMEM((1, TILE), jnp.float32),
            pltpu.VMEM((1, TILE), jnp.float32),
            dma((2, half + 1, 2)),
            dma((2, half + 1, 2)),
            dma((2, half + 1, 2)),
            dma((2, half + 1, 2)),
            dma((1,)),
            dma((1,)),
            dma((peers,)),
            dma((peers,)),
            dma((peers,)),
            dma((peers,)),
            dma((8,)),
        ],
        compiler_params=pltpu.CompilerParams(
            collective_id=0, has_side_effects=True, vmem_limit_bytes=60 * 1024 * 1024
        ),
        cost_estimate=pl.CostEstimate(
            flops=4 * (nq + nd) * n * 4 * width * size,
            bytes_accessed=8 * 1024 * 1024,
            transcendentals=(nq + nd) * n * 4 * width,
        ),
        name="shared_prompt_attention",
    )(
        pq.reshape(nq, size),
        pk.reshape(width, size),
        pv.reshape(width, size),
        dq.reshape(fr, heads, groups, size),
        nk.reshape(fr, heads, size),
        nv.reshape(fr, heads, size),
        ck.reshape(own_rows, slots, size),
        cv.reshape(own_rows, slots, size),
        lens,
    )
    return out.reshape(pq.shape), dec.reshape(dq.shape)


def solution(mesh):
    return jax.shard_map(
        functools.partial(shards, mesh.shape["ctx"], mesh.shape["tp"]),
        mesh=mesh,
        in_specs=(
            P("ctx", "tp", "sec", None),
            P(("ctx", "sec"), "tp", None),
            P(("ctx", "sec"), "tp", None),
            P(("ctx", "sec", "tp"), None, None, None, None),
            P(("ctx", "sec", "tp"), None, None, None),
            P(("ctx", "sec", "tp"), None, None, None),
            P(("ctx", "sec"), None, "tp", None),
            P(("ctx", "sec"), None, "tp", None),
            P(("ctx", "sec")),
        ),
        out_specs=(P("ctx", "tp", "sec", None), P(("ctx", "sec", "tp"), None, None, None, None)),
        check_vma=False,
    )
```

```python
import functools
import math

import jax
import jax.numpy as jnp
from jax import lax
from jax.experimental import pallas as pl
from jax.experimental.pallas import tpu as pltpu
from jax.sharding import PartitionSpec as P

NEG = -1e30
MESH = pl.DeviceIdType.MESH
TILE = 512
ONES = 16


def kernel(
    n, peers, slots, steps, groups, scale2,
    pq_hbm, k_hbm, v_hbm, dq_hbm, nk_hbm, nv_hbm, ck_hbm, cv_hbm, lens_ref,
    out_hbm, dec_hbm,
    kv, qt, acc, top, inbox, outbox, back, ck, cv,
    pq_ref, k_ref, v_ref, dq, nk, nv, pack_ref, score_a, score_b, high_a, high_b,
    out_ref, dec_ref,
    ring_send, ring_recv, sib_send, sib_recv, y_send, y_recv,
    in_send, in_recv, out_send, out_recv, load_sem,
):
    i = lax.axis_index("ctx")
    sec = lax.axis_index("sec")
    tp = lax.axis_index("tp")
    half = n // 2
    h, c = sec // 2, lax.rem(sec, 2)
    right = lax.rem(i + 1, n)
    left = lax.rem(i + n - 1, n)
    to_right, to_left = (right, sec, tp), (left, sec, tp)
    sibling = (i, h * 2 + 1 - c, tp)
    across = (i, (1 - h) * 2 + c, tp)
    width = k_ref.shape[0]
    block = 4 * width
    ptiles = pq_ref.shape[0] // TILE
    dtiles = qt.shape[0] - ptiles
    drows = outbox.shape[1]
    srcs = TILE // drows

    barrier = pltpu.get_barrier_semaphore()
    for device in (to_right, to_left, sibling, across):
        pl.semaphore_signal(barrier, inc=1, device_id=device, device_id_type=MESH)
    for j in range(1, peers):
        device = (i, sec, lax.rem(tp + j, peers))
        pl.semaphore_signal(barrier, inc=1, device_id=device, device_id_type=MESH)

    sources = (k_hbm, v_hbm, dq_hbm, nk_hbm, nv_hbm, pq_hbm, ck_hbm, cv_hbm)
    targets = (k_ref, v_ref, dq, nk, nv, pq_ref, ck, cv)
    loads = [
        pltpu.make_async_copy(source, target, load_sem.at[at])
        for at, (source, target) in enumerate(zip(sources, targets))
    ]
    for load in loads:
        load.start()
    loads[0].wait()
    loads[1].wait()
    kv[i, c, h, 0] = k_ref[...]
    kv[i, c, h, 1] = v_ref[...].astype(jnp.float32).T.astype(jnp.bfloat16)
    pl.semaphore_wait(barrier, 3 + peers)

    def ring(d, s, hh):
        z = lax.rem(i + n - s, n) if d == 0 else lax.rem(i + s, n)
        return pltpu.make_async_remote_copy(
            src_ref=kv.at[z, c, hh],
            dst_ref=kv.at[z, c, hh],
            send_sem=ring_send.at[d, s, hh],
            recv_sem=ring_recv.at[d, s + 1, hh],
            device_id=to_right if d == 0 else to_left,
            device_id_type=MESH,
        )

    def side(d, s, hh, core):
        z = lax.rem(i + n - s, n) if d == 0 else lax.rem(i + s, n)
        return pltpu.make_async_remote_copy(
            src_ref=kv.at[z, core, hh],
            dst_ref=kv.at[z, core, hh],
            send_sem=sib_send.at[d, s, hh],
            recv_sem=sib_recv.at[d, s, hh],
            device_id=sibling,
            device_id_type=MESH,
        )

    def cross(hh):
        return pltpu.make_async_remote_copy(
            src_ref=kv.at[i, c, hh],
            dst_ref=kv.at[i, c, hh],
            send_sem=y_send.at[0],
            recv_sem=y_recv.at[0],
            device_id=across,
            device_id_type=MESH,
        )

    def inward(j):
        to = lax.rem(tp + j, peers)
        return pltpu.make_async_remote_copy(
            src_ref=pack_ref.at[to],
            dst_ref=inbox.at[tp],
            send_sem=in_send.at[j],
            recv_sem=in_recv.at[j],
            device_id=(i, sec, to),
            device_id_type=MESH,
        )

    def inward_wait(j):
        source = lax.rem(tp + peers - j, peers)
        pltpu.make_async_remote_copy(
            src_ref=pack_ref.at[source],
            dst_ref=inbox.at[source],
            send_sem=in_send.at[j],
            recv_sem=in_recv.at[j],
            device_id=(i, sec, source),
            device_id_type=MESH,
        ).wait_recv()

    def outward(j):
        to = lax.rem(tp + j, peers)
        return pltpu.make_async_remote_copy(
            src_ref=outbox.at[to],
            dst_ref=back.at[tp],
            send_sem=out_send.at[j],
            recv_sem=out_recv.at[j],
            device_id=(i, sec, to),
            device_id_type=MESH,
        )

    def outward_wait(j):
        source = lax.rem(tp + peers - j, peers)
        pltpu.make_async_remote_copy(
            src_ref=outbox.at[source],
            dst_ref=back.at[source],
            send_sem=out_send.at[j],
            recv_sem=out_recv.at[j],
            device_id=(i, sec, source),
            device_id_type=MESH,
        ).wait_recv()

    cross(h).start()
    ring(0, 0, h).start()
    ring(1, 0, h).start()
    side(0, 0, h, c).start()
    for at in range(2, 5):
        loads[at].wait()
    queries = jnp.swapaxes(dq[...].astype(jnp.float32), 0, 1).reshape(peers, drows, -1)
    pack_ref[:, :drows, :] = queries.astype(jnp.bfloat16)
    pack_ref[:, drows:, :] = jnp.concatenate(
        [jnp.swapaxes(new[...].astype(jnp.float32), 0, 1) for new in (nk, nv)], axis=1
    ).astype(jnp.bfloat16)
    for j in range(1, peers):
        inward(j).start()
    inbox[tp] = pack_ref[tp]

    def turn_queries(rows):
        return rows.astype(jnp.float32).T.astype(jnp.bfloat16)

    def prepare(t, _):
        qt[t] = turn_queries(pq_ref[pl.ds(pl.multiple_of(t * TILE, TILE), TILE), :])
        return 0

    cross(1 - h).wait_recv()
    ring(0, 0, 1 - h).start()
    ring(1, 0, 1 - h).start()
    side(0, 0, 1 - h, c).start()
    loads[5].wait()
    lax.fori_loop(0, ptiles, prepare, 0)

    def advance(now, later, scores, high, scores_next, high_next, first, mask):
        z, t = now
        best = high[...]
        if not first:
            before = top[t]
            best = jnp.maximum(before, best)
        if later is not None:
            ahead(*later, scores_next, high_next, mask)
        weights = jnp.exp2((scores[...] - best) * scale2).astype(jnp.bfloat16)
        values = jnp.concatenate([kv[z, a, b, 1] for a in range(2) for b in range(2)], axis=1)
        values = jnp.concatenate([values, jnp.ones((ONES, block), jnp.bfloat16)], axis=0)
        mixed = jnp.dot(values, weights, preferred_element_type=jnp.float32)
        if not first:
            mixed = acc[t] * jnp.exp2((before - best) * scale2) + mixed
        acc[t] = mixed
        top[t] = best

    def ahead(z, t, scores, high, mask=None):
        keys = kv[z, :, :, 0].reshape(block, k_ref.shape[1])
        found = jnp.dot(keys, qt[t], preferred_element_type=jnp.float32)
        if mask is not None:
            found = jnp.where(mask(t), found, NEG)
        scores[...] = found
        high[...] = jnp.max(found, axis=0, keepdims=True)

    def lone(z, t, first=False):
        ahead(z, t, score_a, high_a)
        advance((z, t), None, score_a, high_a, None, None, first, None)

    def stream(count, item, first=False, mask=None, hook=None):
        def one(u, _):
            now, second = item(2 * u), item(2 * u + 1)
            later = item(jnp.minimum(2 * u + 2, count - 1))
            if hook is not None:
                pl.when(u == count // 4)(hook)
            advance(now, second, score_a, high_a, score_b, high_b, first, mask)
            advance(second, later, score_b, high_b, score_a, high_a, first, mask)
            return 0

        ahead(*item(0), score_a, high_a, mask)
        lax.fori_loop(0, count // 2, one, 0)

    def causal(t):
        slot = lax.broadcasted_iota(jnp.int32, (block, TILE), 0)
        core, upper = slot // (2 * width), lax.rem(slot // width, 2)
        position = (upper * 2 + core) * width + lax.rem(slot, width)
        query = (t * TILE + lax.broadcasted_iota(jnp.int32, (block, TILE), 1)) // 2
        return position <= query

    def relay(s, order):
        hh = h if order == 0 else 1 - h
        for d in range(2):
            ring(d, s - 1, hh).wait_recv()

            @pl.when((s < half - 1) | (hh == d))
            def _():
                ring(d, s, hh).start()

        for d in range(2):
            side(d, s, hh, c).start()

    relay(jnp.int32(1), 0)
    side(0, 0, 0, 1 - c).wait_recv()
    side(0, 0, 1, 1 - c).wait_recv()
    stream(
        jnp.int32(ptiles), lambda e: (i, e), first=True, mask=causal,
        hook=lambda: relay(jnp.int32(1), 1),
    )

    for j in range(1, peers):
        inward_wait(j)
    for t in range(dtiles):
        rows = inbox[t * srcs : (t + 1) * srcs, :drows, :].reshape(TILE, -1)
        qt[ptiles + t] = turn_queries(rows)

    per = steps * groups
    own = 128 // per
    pairs = 128 // drows
    fresh = (inbox.shape[1] - drows) // 2

    def private(group):
        t, lanes = ptiles + group * 128 // TILE, pl.ds(group * 128 % TILE, 128)
        start = group * own
        queries = qt[t, :, lanes]
        lane_row = lax.broadcasted_iota(jnp.int32, (slots, 128), 1) // per
        limit = jnp.full((slots, 128), lens_ref[start], jnp.int32)
        s_cache = jnp.dot(ck[start], queries, preferred_element_type=jnp.float32)
        for r in range(1, own):
            found = jnp.dot(ck[start + r], queries, preferred_element_type=jnp.float32)
            s_cache = jnp.where(lane_row == r, found, s_cache)
            limit = jnp.where(lane_row == r, lens_ref[start + r], limit)
        slot = lax.broadcasted_iota(jnp.int32, (slots, 128), 0)
        s_cache = jnp.where(slot < limit, s_cache, NEG)
        source = group * pairs
        new_k = jnp.concatenate(
            [inbox[source + b, drows : drows + 2 * fresh, :] for b in range(pairs)], axis=0
        )
        s_new = jnp.dot(new_k, queries, preferred_element_type=jnp.float32)
        shape = (pairs * 2 * fresh, 128)
        key_id = lax.broadcasted_iota(jnp.int32, shape, 0)
        lane = lax.broadcasted_iota(jnp.int32, shape, 1)
        in_pair = lax.rem(key_id, 2 * fresh)
        key_row = key_id // (2 * fresh) * (fresh // steps) + in_pair // steps
        key_step = lax.rem(in_pair, steps)
        ok = (
            (in_pair < fresh)
            & (key_row == lane // per)
            & (key_step <= lax.rem(lane, per) // groups)
        )
        s_new = jnp.where(ok, s_new, NEG)
        before = top[t, :, lanes]
        best = jnp.maximum(
            jnp.max(s_cache, axis=0, keepdims=True), jnp.max(s_new, axis=0, keepdims=True)
        )
        best = jnp.maximum(before, best)
        w_cache = jnp.exp2((s_cache - best) * scale2)
        w_new = jnp.exp2((s_new - best) * scale2)
        sums = jnp.sum(w_cache, axis=0, keepdims=True) + jnp.sum(w_new, axis=0, keepdims=True)
        new_v = jnp.concatenate(
            [
                jnp.roll(
                    inbox[source + b, drows : drows + 2 * fresh, :].astype(jnp.float32),
                    -fresh,
                    axis=0,
                )
                for b in range(pairs)
            ],
            axis=0,
        ).astype(jnp.bfloat16)
        turned = w_cache.T.astype(jnp.bfloat16)
        mixed = jnp.concatenate(
            [
                jnp.dot(
                    turned[r * per : (r + 1) * per],
                    cv[start + r],
                    preferred_element_type=jnp.float32,
                )
                for r in range(own)
            ],
            axis=0,
        ).T + lax.dot_general(
            new_v,
            w_new.astype(jnp.bfloat16),
            (((0,), (0,)), ((), ())),
            preferred_element_type=jnp.float32,
        )
        mixed = jnp.concatenate([mixed, jnp.broadcast_to(sums, (ONES, 128))], axis=0)
        acc[t, :, lanes] = acc[t, :, lanes] * jnp.exp2((before - best) * scale2) + mixed
        top[t, :, lanes] = best

    for t in range(dtiles):
        lone(i, ptiles + t, first=True)
    tiles = ptiles + dtiles

    def work(s, hook=None):
        z_right, z_left = lax.rem(i + n - s, n), lax.rem(i + s, n)
        for d in range(2):
            side(d, s, 0, 1 - c).wait_recv()
            side(d, s, 1, 1 - c).wait_recv()
        low_right = jnp.where(z_right < i, 0, ptiles)
        low_left = jnp.where(z_left < i, 0, ptiles)
        turn = tiles - low_right

        def item(e):
            rightward = e < turn
            z = jnp.where(rightward, z_right, z_left)
            t = jnp.where(rightward, low_right + e, low_left + e - turn)
            return z, t

        stream(turn + tiles - low_left, item, hook=hook)

    relay(jnp.int32(2), 0)
    work(jnp.int32(1), lambda: relay(jnp.int32(2), 1))
    for load in loads[6:]:
        load.wait()
    private_groups = dtiles * TILE // 128

    def step(s, _):
        relay(s, 0)
        for group in range(private_groups):
            pl.when(s == 3 + group)(functools.partial(private, group))
        work(s - 1, lambda: relay(s, 1))
        return 0

    lax.fori_loop(3, half, step, 0)

    work(jnp.int32(half - 1))
    for d in range(2):
        ring(d, half - 1, d).wait_recv()
        side(d, half, d, c).start()
    for d in range(2):
        side(d, half, d, 1 - c).wait_recv()
    z = lax.rem(i + half, n)
    for t in range(dtiles):
        lone(z, ptiles + t)

    depth = acc.shape[1] - ONES
    for t in range(dtiles):
        total = acc[ptiles + t, depth : depth + 1, :]
        rows = (acc[ptiles + t, :depth, :] / total).T.astype(jnp.bfloat16)
        outbox[t * srcs : (t + 1) * srcs] = rows.reshape(srcs, drows, -1)
    for j in range(1, peers):
        outward(j).start()
    back[tp] = outbox[tp]

    @pl.when(z < i)
    def _():
        stream(jnp.int32(ptiles), lambda e: (z, e))

    def finish(t, _):
        total = acc[t, depth : depth + 1, :]
        rows = (acc[t, :depth, :] / total).T.astype(jnp.bfloat16)
        out_ref[pl.ds(pl.multiple_of(t * TILE, TILE), TILE), :] = rows
        return 0

    lax.fori_loop(0, ptiles, finish, 0)
    store = pltpu.make_async_copy(out_ref, out_hbm, load_sem.at[0])
    store.start()

    cross(h).wait_send()
    for hh in range(2):
        side(0, 0, hh, c).wait_send()
        for d in range(2):
            ring(d, 0, hh).wait_send()

    def drain(s, _):
        for hh in range(2):
            for d in range(2):
                side(d, s, hh, c).wait_send()

                @pl.when((s < half - 1) | (hh == d))
                def _():
                    ring(d, s, hh).wait_send()

        return 0

    lax.fori_loop(1, half, drain, 0)
    for d in range(2):
        side(d, half, d, c).wait_send()
    for j in range(1, peers):
        inward(j).wait_send()
    for j in range(1, peers):
        outward_wait(j)
    rows = back[...].astype(jnp.float32).reshape(peers, (drows // groups), groups, -1)
    rows = jnp.swapaxes(rows, 0, 1).reshape((drows // groups), peers * groups, -1)
    dec_ref[...] = rows.astype(jnp.bfloat16)
    give = pltpu.make_async_copy(dec_ref, dec_hbm, load_sem.at[1])
    give.start()
    for j in range(1, peers):
        outward(j).wait_send()
    store.wait()
    give.wait()


def shards(n, peers, pq, pk, pv, dq, nk, nv, ck, cv, lens):
    rows, _, mine, size = pq.shape
    width = pk.shape[0]
    drow, steps, heads, groups, _ = dq.shape
    own_rows, slots = ck.shape[0], ck.shape[1]
    dr = drow * steps * groups
    fr = drow * steps
    nq = rows * mine
    nd = own_rows * steps * groups
    tiles = (nq + nd) // TILE
    half = n // 2
    bf = jnp.bfloat16
    dma = pltpu.SemaphoreType.DMA
    hbm = pl.BlockSpec(memory_space=pl.ANY)
    out, dec = pl.pallas_call(
        functools.partial(
            kernel, n, peers, slots, steps, groups, size**-0.5 * math.log2(math.e)
        ),
        out_shape=(
            jax.ShapeDtypeStruct((nq, size), bf),
            jax.ShapeDtypeStruct((fr, heads * groups, size), bf),
        ),
        in_specs=[hbm] * 8 + [pl.BlockSpec(memory_space=pltpu.SMEM)],
        out_specs=(hbm, hbm),
        scratch_shapes=[
            pltpu.VMEM((n, 2, 2, 2, width, size), bf),
            pltpu.VMEM((tiles, size, TILE), bf),
            pltpu.VMEM((tiles, size + ONES, TILE), jnp.float32),
            pltpu.VMEM((tiles, 1, TILE), jnp.float32),
            pltpu.VMEM((peers, dr + 2 * fr, size), bf),
            pltpu.VMEM((peers, dr, size), bf),
            pltpu.VMEM((peers, dr, size), bf),
            pltpu.VMEM((own_rows, slots, size), bf),
            pltpu.VMEM((own_rows, slots, size), bf),
            pltpu.VMEM((nq, size), bf),
            pltpu.VMEM((width, size), bf),
            pltpu.VMEM((width, size), bf),
            pltpu.VMEM((fr, heads, groups, size), bf),
            pltpu.VMEM((fr, heads, size), bf),
            pltpu.VMEM((fr, heads, size), bf),
            pltpu.VMEM((peers, dr + 2 * fr, size), bf),
            pltpu.VMEM((4 * width, TILE), jnp.float32),
            pltpu.VMEM((4 * width, TILE), jnp.float32),
            pltpu.VMEM((1, TILE), jnp.float32),
            pltpu.VMEM((1, TILE), jnp.float32),
            pltpu.VMEM((nq, size), bf),
            pltpu.VMEM((fr, heads * groups, size), bf),
            dma((2, half + 1, 2)),
            dma((2, half + 1, 2)),
            dma((2, half + 1, 2)),
            dma((2, half + 1, 2)),
            dma((1,)),
            dma((1,)),
            dma((peers,)),
            dma((peers,)),
            dma((peers,)),
            dma((peers,)),
            dma((8,)),
        ],
        compiler_params=pltpu.CompilerParams(
            collective_id=0, has_side_effects=True, vmem_limit_bytes=60 * 1024 * 1024
        ),
        cost_estimate=pl.CostEstimate(
            flops=4 * (nq + nd) * n * 4 * width * size,
            bytes_accessed=8 * 1024 * 1024,
            transcendentals=(nq + nd) * n * 4 * width,
        ),
        name="shared_prompt_attention",
    )(
        pq.reshape(nq, size),
        pk.reshape(width, size),
        pv.reshape(width, size),
        dq.reshape(fr, heads, groups, size),
        nk.reshape(fr, heads, size),
        nv.reshape(fr, heads, size),
        ck.reshape(own_rows, slots, size),
        cv.reshape(own_rows, slots, size),
        lens,
    )
    return out.reshape(pq.shape), dec.reshape(dq.shape)


def solution(mesh):
    return jax.shard_map(
        functools.partial(shards, mesh.shape["ctx"], mesh.shape["tp"]),
        mesh=mesh,
        in_specs=(
            P("ctx", "tp", "sec", None),
            P(("ctx", "sec"), "tp", None),
            P(("ctx", "sec"), "tp", None),
            P(("ctx", "sec", "tp"), None, None, None, None),
            P(("ctx", "sec", "tp"), None, None, None),
            P(("ctx", "sec", "tp"), None, None, None),
            P(("ctx", "sec"), None, "tp", None),
            P(("ctx", "sec"), None, "tp", None),
            P(("ctx", "sec")),
        ),
        out_specs=(P("ctx", "tp", "sec", None), P(("ctx", "sec", "tp"), None, None, None, None)),
        check_vma=False,
    )
```

```python
import functools
import math

import jax
import jax.numpy as jnp
from jax import lax
from jax.experimental import pallas as pl
from jax.experimental.pallas import tpu as pltpu
from jax.sharding import PartitionSpec as P

NEG = -1e30
MESH = pl.DeviceIdType.MESH
TILE = 512
ONES = 16


def kernel(
    n, peers, slots, steps, groups, scale2,
    pq_hbm, k_hbm, v_hbm, dq_hbm, nk_hbm, nv_hbm, ck_hbm, cv_hbm, lens_ref,
    out_hbm, dec_hbm,
    kv, qt, acc, top, inbox, outbox, back, ck, cv,
    pq_ref, k_ref, v_ref, dq, nk, nv, pack_ref, score_a, score_b, high_a, high_b,
    out_ref, dec_ref,
    ring_send, ring_recv, sib_send, sib_recv, y_send, y_recv,
    in_send, in_recv, out_send, out_recv, load_sem,
):
    i = lax.axis_index("ctx")
    sec = lax.axis_index("sec")
    tp = lax.axis_index("tp")
    half = n // 2
    h, c = sec // 2, lax.rem(sec, 2)
    right = lax.rem(i + 1, n)
    left = lax.rem(i + n - 1, n)
    to_right, to_left = (right, sec, tp), (left, sec, tp)
    sibling = (i, h * 2 + 1 - c, tp)
    across = (i, (1 - h) * 2 + c, tp)
    width = k_ref.shape[0]
    block = 4 * width
    ptiles = pq_ref.shape[0] // TILE
    dtiles = qt.shape[0] - ptiles
    drows = outbox.shape[1]
    srcs = TILE // drows

    barrier = pltpu.get_barrier_semaphore()
    for device in (to_right, to_left, sibling, across):
        pl.semaphore_signal(barrier, inc=1, device_id=device, device_id_type=MESH)
    for j in range(1, peers):
        device = (i, sec, lax.rem(tp + j, peers))
        pl.semaphore_signal(barrier, inc=1, device_id=device, device_id_type=MESH)

    sources = (k_hbm, v_hbm, dq_hbm, nk_hbm, nv_hbm, pq_hbm, ck_hbm, cv_hbm)
    targets = (k_ref, v_ref, dq, nk, nv, pq_ref, ck, cv)
    loads = [
        pltpu.make_async_copy(source, target, load_sem.at[at])
        for at, (source, target) in enumerate(zip(sources, targets))
    ]
    for load in loads:
        load.start()
    loads[0].wait()
    loads[1].wait()
    kv[i, c, h, 0] = k_ref[...]
    kv[i, c, h, 1] = v_ref[...].astype(jnp.float32).T.astype(jnp.bfloat16)
    pl.semaphore_wait(barrier, 3 + peers)

    sign = 1 - 2 * c
    onward = (jnp.where(c == 0, right, left), sec, tp)

    def mine(s):
        return lax.rem(i + n - s * sign, n)

    def theirs(s):
        return lax.rem(i + n + s * sign, n)

    def ring(s, cc, hh):
        return pltpu.make_async_remote_copy(
            src_ref=kv.at[mine(s), cc, hh],
            dst_ref=kv.at[mine(s), cc, hh],
            send_sem=ring_send.at[s, cc, hh],
            recv_sem=ring_recv.at[s + 1, cc, hh],
            device_id=onward,
            device_id_type=MESH,
        )

    def side(s, cc, hh, z=None):
        z = mine(s) if z is None else z
        return pltpu.make_async_remote_copy(
            src_ref=kv.at[z, cc, hh],
            dst_ref=kv.at[z, cc, hh],
            send_sem=sib_send.at[s, cc, hh],
            recv_sem=sib_recv.at[s, cc, hh],
            device_id=sibling,
            device_id_type=MESH,
        )

    def side_wait(s, cc, hh):
        side(s, cc, hh, theirs(s)).wait_recv()

    def landed(s, cc, hh):
        pltpu.make_async_remote_copy(
            src_ref=kv.at[mine(s), cc, hh],
            dst_ref=kv.at[mine(s), cc, hh],
            send_sem=ring_send.at[s - 1, cc, hh],
            recv_sem=ring_recv.at[s, cc, hh],
            device_id=onward,
            device_id_type=MESH,
        ).wait_recv()

    def cross(hh):
        return pltpu.make_async_remote_copy(
            src_ref=kv.at[i, c, hh],
            dst_ref=kv.at[i, c, hh],
            send_sem=y_send.at[0],
            recv_sem=y_recv.at[0],
            device_id=across,
            device_id_type=MESH,
        )

    def inward(j):
        to = lax.rem(tp + j, peers)
        return pltpu.make_async_remote_copy(
            src_ref=pack_ref.at[to],
            dst_ref=inbox.at[tp],
            send_sem=in_send.at[j],
            recv_sem=in_recv.at[j],
            device_id=(i, sec, to),
            device_id_type=MESH,
        )

    def inward_wait(j):
        source = lax.rem(tp + peers - j, peers)
        pltpu.make_async_remote_copy(
            src_ref=pack_ref.at[source],
            dst_ref=inbox.at[source],
            send_sem=in_send.at[j],
            recv_sem=in_recv.at[j],
            device_id=(i, sec, source),
            device_id_type=MESH,
        ).wait_recv()

    def outward(j):
        to = lax.rem(tp + j, peers)
        return pltpu.make_async_remote_copy(
            src_ref=outbox.at[to],
            dst_ref=back.at[tp],
            send_sem=out_send.at[j],
            recv_sem=out_recv.at[j],
            device_id=(i, sec, to),
            device_id_type=MESH,
        )

    def outward_wait(j):
        source = lax.rem(tp + peers - j, peers)
        pltpu.make_async_remote_copy(
            src_ref=outbox.at[source],
            dst_ref=back.at[source],
            send_sem=out_send.at[j],
            recv_sem=out_recv.at[j],
            device_id=(i, sec, source),
            device_id_type=MESH,
        ).wait_recv()

    ring(0, c, h).start()
    cross(h).start()
    side(0, c, h).start()
    for at in range(2, 5):
        loads[at].wait()
    queries = jnp.swapaxes(dq[...].astype(jnp.float32), 0, 1).reshape(peers, drows, -1)
    pack_ref[:, :drows, :] = queries.astype(jnp.bfloat16)
    pack_ref[:, drows:, :] = jnp.concatenate(
        [jnp.swapaxes(new[...].astype(jnp.float32), 0, 1) for new in (nk, nv)], axis=1
    ).astype(jnp.bfloat16)
    for j in range(1, peers):
        inward(j).start()
    inbox[tp] = pack_ref[tp]

    def turn_queries(rows):
        return rows.astype(jnp.float32).T.astype(jnp.bfloat16)

    def prepare(t, _):
        qt[t] = turn_queries(pq_ref[pl.ds(pl.multiple_of(t * TILE, TILE), TILE), :])
        return 0

    side_wait(0, 1 - c, h)
    ring(0, 1 - c, h).start()
    cross(1 - h).wait_recv()
    ring(0, c, 1 - h).start()
    side(0, c, 1 - h).start()
    side_wait(0, 1 - c, 1 - h)
    ring(0, 1 - c, 1 - h).start()
    loads[5].wait()
    lax.fori_loop(0, ptiles, prepare, 0)

    def advance(now, later, scores, high, scores_next, high_next, first, mask):
        z, t = now
        best = high[...]
        if not first:
            before = top[t]
            best = jnp.maximum(before, best)
        if later is not None:
            ahead(*later, scores_next, high_next, mask)
        weights = jnp.exp2((scores[...] - best) * scale2).astype(jnp.bfloat16)
        values = jnp.concatenate([kv[z, a, b, 1] for a in range(2) for b in range(2)], axis=1)
        values = jnp.concatenate([values, jnp.ones((ONES, block), jnp.bfloat16)], axis=0)
        mixed = jnp.dot(values, weights, preferred_element_type=jnp.float32)
        if not first:
            mixed = acc[t] * jnp.exp2((before - best) * scale2) + mixed
        acc[t] = mixed
        top[t] = best

    def ahead(z, t, scores, high, mask=None):
        keys = kv[z, :, :, 0].reshape(block, k_ref.shape[1])
        found = jnp.dot(keys, qt[t], preferred_element_type=jnp.float32)
        if mask is not None:
            found = jnp.where(mask(t), found, NEG)
        scores[...] = found
        high[...] = jnp.max(found, axis=0, keepdims=True)

    def lone(z, t, first=False):
        ahead(z, t, score_a, high_a)
        advance((z, t), None, score_a, high_a, None, None, first, None)

    def stream(count, item, first=False, mask=None, hook=None):
        def one(u, _):
            now, second = item(2 * u), item(2 * u + 1)
            later = item(jnp.minimum(2 * u + 2, count - 1))
            if hook is not None:
                pl.when(u == count // 4)(hook)
            advance(now, second, score_a, high_a, score_b, high_b, first, mask)
            advance(second, later, score_b, high_b, score_a, high_a, first, mask)
            return 0

        ahead(*item(0), score_a, high_a, mask)
        lax.fori_loop(0, count // 2, one, 0)

    def causal(t):
        slot = lax.broadcasted_iota(jnp.int32, (block, TILE), 0)
        core, upper = slot // (2 * width), lax.rem(slot // width, 2)
        position = (upper * 2 + core) * width + lax.rem(slot, width)
        query = (t * TILE + lax.broadcasted_iota(jnp.int32, (block, TILE), 1)) // 2
        return position <= query

    def relay(s, order):
        hh = h if order == 0 else 1 - h
        for cc in (c, 1 - c):
            landed(s, cc, hh)

            @pl.when((s < half - 1) | (hh == c))
            def _():
                ring(s, cc, hh).start()

            side(s, cc, hh).start()

    relay(jnp.int32(1), 0)
    stream(
        jnp.int32(ptiles), lambda e: (i, e), first=True, mask=causal,
        hook=lambda: relay(jnp.int32(1), 1),
    )

    for j in range(1, peers):
        inward_wait(j)
    for t in range(dtiles):
        rows = inbox[t * srcs : (t + 1) * srcs, :drows, :].reshape(TILE, -1)
        qt[ptiles + t] = turn_queries(rows)

    per = steps * groups
    own = 128 // per
    pairs = 128 // drows
    fresh = (inbox.shape[1] - drows) // 2

    def private(group):
        t, lanes = ptiles + group * 128 // TILE, pl.ds(group * 128 % TILE, 128)
        start = group * own
        queries = qt[t, :, lanes]
        lane_row = lax.broadcasted_iota(jnp.int32, (slots, 128), 1) // per
        limit = jnp.full((slots, 128), lens_ref[start], jnp.int32)
        s_cache = jnp.dot(ck[start], queries, preferred_element_type=jnp.float32)
        for r in range(1, own):
            found = jnp.dot(ck[start + r], queries, preferred_element_type=jnp.float32)
            s_cache = jnp.where(lane_row == r, found, s_cache)
            limit = jnp.where(lane_row == r, lens_ref[start + r], limit)
        slot = lax.broadcasted_iota(jnp.int32, (slots, 128), 0)
        s_cache = jnp.where(slot < limit, s_cache, NEG)
        source = group * pairs
        new_k = jnp.concatenate(
            [inbox[source + b, drows : drows + 2 * fresh, :] for b in range(pairs)], axis=0
        )
        s_new = jnp.dot(new_k, queries, preferred_element_type=jnp.float32)
        shape = (pairs * 2 * fresh, 128)
        key_id = lax.broadcasted_iota(jnp.int32, shape, 0)
        lane = lax.broadcasted_iota(jnp.int32, shape, 1)
        in_pair = lax.rem(key_id, 2 * fresh)
        key_row = key_id // (2 * fresh) * (fresh // steps) + in_pair // steps
        key_step = lax.rem(in_pair, steps)
        ok = (
            (in_pair < fresh)
            & (key_row == lane // per)
            & (key_step <= lax.rem(lane, per) // groups)
        )
        s_new = jnp.where(ok, s_new, NEG)
        before = top[t, :, lanes]
        best = jnp.maximum(
            jnp.max(s_cache, axis=0, keepdims=True), jnp.max(s_new, axis=0, keepdims=True)
        )
        best = jnp.maximum(before, best)
        w_cache = jnp.exp2((s_cache - best) * scale2)
        w_new = jnp.exp2((s_new - best) * scale2)
        sums = jnp.sum(w_cache, axis=0, keepdims=True) + jnp.sum(w_new, axis=0, keepdims=True)
        new_v = jnp.concatenate(
            [
                jnp.roll(
                    inbox[source + b, drows : drows + 2 * fresh, :].astype(jnp.float32),
                    -fresh,
                    axis=0,
                )
                for b in range(pairs)
            ],
            axis=0,
        ).astype(jnp.bfloat16)
        turned = w_cache.T.astype(jnp.bfloat16)
        mixed = jnp.concatenate(
            [
                jnp.dot(
                    turned[r * per : (r + 1) * per],
                    cv[start + r],
                    preferred_element_type=jnp.float32,
                )
                for r in range(own)
            ],
            axis=0,
        ).T + lax.dot_general(
            new_v,
            w_new.astype(jnp.bfloat16),
            (((0,), (0,)), ((), ())),
            preferred_element_type=jnp.float32,
        )
        mixed = jnp.concatenate([mixed, jnp.broadcast_to(sums, (ONES, 128))], axis=0)
        acc[t, :, lanes] = acc[t, :, lanes] * jnp.exp2((before - best) * scale2) + mixed
        top[t, :, lanes] = best

    for t in range(dtiles):
        lone(i, ptiles + t, first=True)
    tiles = ptiles + dtiles

    def work(s, hook=None):
        z_right, z_left = mine(s), theirs(s)
        for cc in range(2):
            for hh in range(2):
                side_wait(s, cc, hh)
        low_right = jnp.where(z_right < i, 0, ptiles)
        low_left = jnp.where(z_left < i, 0, ptiles)
        turn = tiles - low_right

        def item(e):
            rightward = e < turn
            z = jnp.where(rightward, z_right, z_left)
            t = jnp.where(rightward, low_right + e, low_left + e - turn)
            return z, t

        stream(turn + tiles - low_left, item, hook=hook)

    relay(jnp.int32(2), 0)
    work(jnp.int32(1), lambda: relay(jnp.int32(2), 1))
    for load in loads[6:]:
        load.wait()
    private_groups = dtiles * TILE // 128

    def step(s, _):
        relay(s, 0)
        for group in range(private_groups):
            pl.when(s == 3 + group)(functools.partial(private, group))
        work(s - 1, lambda: relay(s, 1))
        return 0

    lax.fori_loop(3, half, step, 0)

    work(jnp.int32(half - 1))
    for cc in range(2):
        landed(half, cc, c)
        side(half, cc, c).start()
    for cc in range(2):
        side_wait(half, cc, 1 - c)
    z = lax.rem(i + half, n)
    for t in range(dtiles):
        lone(z, ptiles + t)

    depth = acc.shape[1] - ONES
    for t in range(dtiles):
        total = acc[ptiles + t, depth : depth + 1, :]
        rows = (acc[ptiles + t, :depth, :] / total).T.astype(jnp.bfloat16)
        outbox[t * srcs : (t + 1) * srcs] = rows.reshape(srcs, drows, -1)
    for j in range(1, peers):
        outward(j).start()
    back[tp] = outbox[tp]

    @pl.when(z < i)
    def _():
        stream(jnp.int32(ptiles), lambda e: (z, e))

    def finish(t, _):
        total = acc[t, depth : depth + 1, :]
        rows = (acc[t, :depth, :] / total).T.astype(jnp.bfloat16)
        out_ref[pl.ds(pl.multiple_of(t * TILE, TILE), TILE), :] = rows
        return 0

    lax.fori_loop(0, ptiles, finish, 0)
    store = pltpu.make_async_copy(out_ref, out_hbm, load_sem.at[0])
    store.start()

    cross(h).wait_send()
    for hh in range(2):
        side(0, c, hh).wait_send()
        for cc in range(2):
            ring(0, cc, hh).wait_send()

    def drain(s, _):
        for hh in range(2):
            for cc in range(2):
                side(s, cc, hh).wait_send()

                @pl.when((s < half - 1) | (hh == c))
                def _():
                    ring(s, cc, hh).wait_send()

        return 0

    lax.fori_loop(1, half, drain, 0)
    for cc in range(2):
        side(half, cc, c).wait_send()
    for j in range(1, peers):
        inward(j).wait_send()
    for j in range(1, peers):
        outward_wait(j)
    rows = back[...].astype(jnp.float32).reshape(peers, (drows // groups), groups, -1)
    rows = jnp.swapaxes(rows, 0, 1).reshape((drows // groups), peers * groups, -1)
    dec_ref[...] = rows.astype(jnp.bfloat16)
    give = pltpu.make_async_copy(dec_ref, dec_hbm, load_sem.at[1])
    give.start()
    for j in range(1, peers):
        outward(j).wait_send()
    store.wait()
    give.wait()


def shards(n, peers, pq, pk, pv, dq, nk, nv, ck, cv, lens):
    rows, _, mine, size = pq.shape
    width = pk.shape[0]
    drow, steps, heads, groups, _ = dq.shape
    own_rows, slots = ck.shape[0], ck.shape[1]
    dr = drow * steps * groups
    fr = drow * steps
    nq = rows * mine
    nd = own_rows * steps * groups
    tiles = (nq + nd) // TILE
    half = n // 2
    bf = jnp.bfloat16
    dma = pltpu.SemaphoreType.DMA
    hbm = pl.BlockSpec(memory_space=pl.ANY)
    out, dec = pl.pallas_call(
        functools.partial(
            kernel, n, peers, slots, steps, groups, size**-0.5 * math.log2(math.e)
        ),
        out_shape=(
            jax.ShapeDtypeStruct((nq, size), bf),
            jax.ShapeDtypeStruct((fr, heads * groups, size), bf),
        ),
        in_specs=[hbm] * 8 + [pl.BlockSpec(memory_space=pltpu.SMEM)],
        out_specs=(hbm, hbm),
        scratch_shapes=[
            pltpu.VMEM((n, 2, 2, 2, width, size), bf),
            pltpu.VMEM((tiles, size, TILE), bf),
            pltpu.VMEM((tiles, size + ONES, TILE), jnp.float32),
            pltpu.VMEM((tiles, 1, TILE), jnp.float32),
            pltpu.VMEM((peers, dr + 2 * fr, size), bf),
            pltpu.VMEM((peers, dr, size), bf),
            pltpu.VMEM((peers, dr, size), bf),
            pltpu.VMEM((own_rows, slots, size), bf),
            pltpu.VMEM((own_rows, slots, size), bf),
            pltpu.VMEM((nq, size), bf),
            pltpu.VMEM((width, size), bf),
            pltpu.VMEM((width, size), bf),
            pltpu.VMEM((fr, heads, groups, size), bf),
            pltpu.VMEM((fr, heads, size), bf),
            pltpu.VMEM((fr, heads, size), bf),
            pltpu.VMEM((peers, dr + 2 * fr, size), bf),
            pltpu.VMEM((4 * width, TILE), jnp.float32),
            pltpu.VMEM((4 * width, TILE), jnp.float32),
            pltpu.VMEM((1, TILE), jnp.float32),
            pltpu.VMEM((1, TILE), jnp.float32),
            pltpu.VMEM((nq, size), bf),
            pltpu.VMEM((fr, heads * groups, size), bf),
            dma((half + 1, 2, 2)),
            dma((half + 1, 2, 2)),
            dma((half + 1, 2, 2)),
            dma((half + 1, 2, 2)),
            dma((1,)),
            dma((1,)),
            dma((peers,)),
            dma((peers,)),
            dma((peers,)),
            dma((peers,)),
            dma((8,)),
        ],
        compiler_params=pltpu.CompilerParams(
            collective_id=0, has_side_effects=True, vmem_limit_bytes=60 * 1024 * 1024
        ),
        cost_estimate=pl.CostEstimate(
            flops=4 * (nq + nd) * n * 4 * width * size,
            bytes_accessed=8 * 1024 * 1024,
            transcendentals=(nq + nd) * n * 4 * width,
        ),
        name="shared_prompt_attention",
    )(
        pq.reshape(nq, size),
        pk.reshape(width, size),
        pv.reshape(width, size),
        dq.reshape(fr, heads, groups, size),
        nk.reshape(fr, heads, size),
        nv.reshape(fr, heads, size),
        ck.reshape(own_rows, slots, size),
        cv.reshape(own_rows, slots, size),
        lens,
    )
    return out.reshape(pq.shape), dec.reshape(dq.shape)


def solution(mesh):
    return jax.shard_map(
        functools.partial(shards, mesh.shape["ctx"], mesh.shape["tp"]),
        mesh=mesh,
        in_specs=(
            P("ctx", "tp", "sec", None),
            P(("ctx", "sec"), "tp", None),
            P(("ctx", "sec"), "tp", None),
            P(("ctx", "sec", "tp"), None, None, None, None),
            P(("ctx", "sec", "tp"), None, None, None),
            P(("ctx", "sec", "tp"), None, None, None),
            P(("ctx", "sec"), None, "tp", None),
            P(("ctx", "sec"), None, "tp", None),
            P(("ctx", "sec")),
        ),
        out_specs=(P("ctx", "tp", "sec", None), P(("ctx", "sec", "tp"), None, None, None, None)),
        check_vma=False,
    )
```

```python
import functools
import math

import jax
import jax.numpy as jnp
from jax import lax
from jax.experimental import pallas as pl
from jax.experimental.pallas import tpu as pltpu
from jax.sharding import PartitionSpec as P

NEG = -1e30
MESH = pl.DeviceIdType.MESH
TILE = 512
ONES = 16


def kernel(
    n, peers, slots, steps, groups, scale2,
    pq_hbm, k_hbm, v_hbm, dq_hbm, nk_hbm, nv_hbm, ck_hbm, cv_hbm, lens_ref,
    out_hbm, dec_hbm,
    kv, qt, acc, top, inbox, outbox, back, ck, cv,
    pq_ref, k_ref, v_ref, dq, nk, nv, pack_ref, score_a, score_b, high_a, high_b,
    out_ref, dec_ref,
    ring_send, ring_recv, sib_send, sib_recv, y_send, y_recv,
    in_send, in_recv, out_send, out_recv, load_sem,
):
    i = lax.axis_index("ctx")
    sec = lax.axis_index("sec")
    tp = lax.axis_index("tp")
    half = n // 2
    h, c = sec // 2, lax.rem(sec, 2)
    right = lax.rem(i + 1, n)
    left = lax.rem(i + n - 1, n)
    to_right, to_left = (right, sec, tp), (left, sec, tp)
    sibling = (i, h * 2 + 1 - c, tp)
    across = (i, (1 - h) * 2 + c, tp)
    width = k_ref.shape[0]
    block = 4 * width
    ptiles = pq_ref.shape[0] // TILE
    dtiles = qt.shape[0] - ptiles
    drows = outbox.shape[1]
    srcs = TILE // drows

    barrier = pltpu.get_barrier_semaphore()
    for device in (to_right, to_left, sibling, across):
        pl.semaphore_signal(barrier, inc=1, device_id=device, device_id_type=MESH)
    for j in range(1, peers):
        device = (i, sec, lax.rem(tp + j, peers))
        pl.semaphore_signal(barrier, inc=1, device_id=device, device_id_type=MESH)

    sources = (k_hbm, v_hbm, dq_hbm, nk_hbm, nv_hbm, pq_hbm, ck_hbm, cv_hbm)
    targets = (k_ref, v_ref, dq, nk, nv, pq_ref, ck, cv)
    loads = [
        pltpu.make_async_copy(source, target, load_sem.at[at])
        for at, (source, target) in enumerate(zip(sources, targets))
    ]
    for load in loads:
        load.start()
    loads[0].wait()
    loads[1].wait()
    kv[i, c, h, 0] = k_ref[...]
    kv[i, c, h, 1] = v_ref[...].astype(jnp.float32).T.astype(jnp.bfloat16)
    pl.semaphore_wait(barrier, 3 + peers)

    sign = 1 - 2 * c
    onward = (jnp.where(c == 0, right, left), sec, tp)

    def mine(s):
        return lax.rem(i + n - s * sign, n)

    def theirs(s):
        return lax.rem(i + n + s * sign, n)

    def ring(s, cc, hh):
        return pltpu.make_async_remote_copy(
            src_ref=kv.at[mine(s), cc, hh],
            dst_ref=kv.at[mine(s), cc, hh],
            send_sem=ring_send.at[s, cc, hh],
            recv_sem=ring_recv.at[s + 1, cc, hh],
            device_id=onward,
            device_id_type=MESH,
        )

    def side(s, cc, hh, z=None):
        z = mine(s) if z is None else z
        return pltpu.make_async_remote_copy(
            src_ref=kv.at[z, cc, hh],
            dst_ref=kv.at[z, cc, hh],
            send_sem=sib_send.at[s, cc, hh],
            recv_sem=sib_recv.at[s, cc, hh],
            device_id=sibling,
            device_id_type=MESH,
        )

    def side_wait(s, cc, hh):
        side(s, cc, hh, theirs(s)).wait_recv()

    def landed(s, cc, hh):
        pltpu.make_async_remote_copy(
            src_ref=kv.at[mine(s), cc, hh],
            dst_ref=kv.at[mine(s), cc, hh],
            send_sem=ring_send.at[s - 1, cc, hh],
            recv_sem=ring_recv.at[s, cc, hh],
            device_id=onward,
            device_id_type=MESH,
        ).wait_recv()

    def cross(hh):
        return pltpu.make_async_remote_copy(
            src_ref=kv.at[i, c, hh],
            dst_ref=kv.at[i, c, hh],
            send_sem=y_send.at[0],
            recv_sem=y_recv.at[0],
            device_id=across,
            device_id_type=MESH,
        )

    def inward(j):
        to = lax.rem(tp + j, peers)
        return pltpu.make_async_remote_copy(
            src_ref=pack_ref.at[to],
            dst_ref=inbox.at[tp],
            send_sem=in_send.at[j],
            recv_sem=in_recv.at[j],
            device_id=(i, sec, to),
            device_id_type=MESH,
        )

    def inward_wait(j):
        source = lax.rem(tp + peers - j, peers)
        pltpu.make_async_remote_copy(
            src_ref=pack_ref.at[source],
            dst_ref=inbox.at[source],
            send_sem=in_send.at[j],
            recv_sem=in_recv.at[j],
            device_id=(i, sec, source),
            device_id_type=MESH,
        ).wait_recv()

    def outward(j):
        to = lax.rem(tp + j, peers)
        return pltpu.make_async_remote_copy(
            src_ref=outbox.at[to],
            dst_ref=back.at[tp],
            send_sem=out_send.at[j],
            recv_sem=out_recv.at[j],
            device_id=(i, sec, to),
            device_id_type=MESH,
        )

    def outward_wait(j):
        source = lax.rem(tp + peers - j, peers)
        pltpu.make_async_remote_copy(
            src_ref=outbox.at[source],
            dst_ref=back.at[source],
            send_sem=out_send.at[j],
            recv_sem=out_recv.at[j],
            device_id=(i, sec, source),
            device_id_type=MESH,
        ).wait_recv()

    ring(0, c, h).start()
    cross(h).start()
    side(0, c, h).start()
    for at in range(2, 5):
        loads[at].wait()
    queries = jnp.swapaxes(dq[...].astype(jnp.float32), 0, 1).reshape(peers, drows, -1)
    pack_ref[:, :drows, :] = queries.astype(jnp.bfloat16)
    pack_ref[:, drows:, :] = jnp.concatenate(
        [jnp.swapaxes(new[...].astype(jnp.float32), 0, 1) for new in (nk, nv)], axis=1
    ).astype(jnp.bfloat16)
    for j in range(1, peers):
        inward(j).start()
    inbox[tp] = pack_ref[tp]

    def turn_queries(rows):
        return rows.astype(jnp.float32).T.astype(jnp.bfloat16)

    def prepare(t, _):
        qt[t] = turn_queries(pq_ref[pl.ds(pl.multiple_of(t * TILE, TILE), TILE), :])
        return 0

    side_wait(0, 1 - c, h)
    ring(0, 1 - c, h).start()
    cross(1 - h).wait_recv()
    ring(0, c, 1 - h).start()
    side(0, c, 1 - h).start()
    side_wait(0, 1 - c, 1 - h)
    ring(0, 1 - c, 1 - h).start()
    loads[5].wait()
    lax.fori_loop(0, ptiles, prepare, 0)

    def advance(now, later, scores, high, scores_next, high_next, first, mask):
        z, t = now
        best = high[...]
        if not first:
            before = top[t]
            best = jnp.maximum(before, best)
        if later is not None:
            ahead(*later, scores_next, high_next, mask)
        weights = jnp.exp2(((scores[...] - best) * scale2).astype(jnp.bfloat16))
        values = jnp.concatenate([kv[z, a, b, 1] for a in range(2) for b in range(2)], axis=1)
        values = jnp.concatenate([values, jnp.ones((ONES, block), jnp.bfloat16)], axis=0)
        mixed = jnp.dot(values, weights, preferred_element_type=jnp.float32)
        if not first:
            mixed = acc[t] * jnp.exp2((before - best) * scale2) + mixed
        acc[t] = mixed
        top[t] = best

    def ahead(z, t, scores, high, mask=None):
        keys = kv[z, :, :, 0].reshape(block, k_ref.shape[1])
        found = jnp.dot(keys, qt[t], preferred_element_type=jnp.float32)
        if mask is not None:
            found = jnp.where(mask(t), found, NEG)
        scores[...] = found
        high[...] = jnp.max(found, axis=0, keepdims=True)

    def lone(z, t, first=False):
        ahead(z, t, score_a, high_a)
        advance((z, t), None, score_a, high_a, None, None, first, None)

    def stream(count, item, first=False, mask=None, hook=None):
        def one(u, _):
            now, second = item(2 * u), item(2 * u + 1)
            later = item(jnp.minimum(2 * u + 2, count - 1))
            if hook is not None:
                pl.when(u == count // 4)(hook)
            advance(now, second, score_a, high_a, score_b, high_b, first, mask)
            advance(second, later, score_b, high_b, score_a, high_a, first, mask)
            return 0

        ahead(*item(0), score_a, high_a, mask)
        lax.fori_loop(0, count // 2, one, 0)

    def causal(t):
        slot = lax.broadcasted_iota(jnp.int32, (block, TILE), 0)
        core, upper = slot // (2 * width), lax.rem(slot // width, 2)
        position = (upper * 2 + core) * width + lax.rem(slot, width)
        query = (t * TILE + lax.broadcasted_iota(jnp.int32, (block, TILE), 1)) // 2
        return position <= query

    def relay(s, order):
        hh = h if order == 0 else 1 - h
        for cc in (c, 1 - c):
            landed(s, cc, hh)

            @pl.when((s < half - 1) | (hh == c))
            def _():
                ring(s, cc, hh).start()

            side(s, cc, hh).start()

    relay(jnp.int32(1), 0)
    stream(
        jnp.int32(ptiles), lambda e: (i, e), first=True, mask=causal,
        hook=lambda: relay(jnp.int32(1), 1),
    )

    for j in range(1, peers):
        inward_wait(j)
    for t in range(dtiles):
        rows = inbox[t * srcs : (t + 1) * srcs, :drows, :].reshape(TILE, -1)
        qt[ptiles + t] = turn_queries(rows)

    per = steps * groups
    own = 128 // per
    pairs = 128 // drows
    fresh = (inbox.shape[1] - drows) // 2

    def private(group):
        t, lanes = ptiles + group * 128 // TILE, pl.ds(group * 128 % TILE, 128)
        start = group * own
        queries = qt[t, :, lanes]
        lane_row = lax.broadcasted_iota(jnp.int32, (slots, 128), 1) // per
        limit = jnp.full((slots, 128), lens_ref[start], jnp.int32)
        s_cache = jnp.dot(ck[start], queries, preferred_element_type=jnp.float32)
        for r in range(1, own):
            found = jnp.dot(ck[start + r], queries, preferred_element_type=jnp.float32)
            s_cache = jnp.where(lane_row == r, found, s_cache)
            limit = jnp.where(lane_row == r, lens_ref[start + r], limit)
        slot = lax.broadcasted_iota(jnp.int32, (slots, 128), 0)
        s_cache = jnp.where(slot < limit, s_cache, NEG)
        source = group * pairs
        new_k = jnp.concatenate(
            [inbox[source + b, drows : drows + 2 * fresh, :] for b in range(pairs)], axis=0
        )
        s_new = jnp.dot(new_k, queries, preferred_element_type=jnp.float32)
        shape = (pairs * 2 * fresh, 128)
        key_id = lax.broadcasted_iota(jnp.int32, shape, 0)
        lane = lax.broadcasted_iota(jnp.int32, shape, 1)
        in_pair = lax.rem(key_id, 2 * fresh)
        key_row = key_id // (2 * fresh) * (fresh // steps) + in_pair // steps
        key_step = lax.rem(in_pair, steps)
        ok = (
            (in_pair < fresh)
            & (key_row == lane // per)
            & (key_step <= lax.rem(lane, per) // groups)
        )
        s_new = jnp.where(ok, s_new, NEG)
        before = top[t, :, lanes]
        best = jnp.maximum(
            jnp.max(s_cache, axis=0, keepdims=True), jnp.max(s_new, axis=0, keepdims=True)
        )
        best = jnp.maximum(before, best)
        w_cache = jnp.exp2((s_cache - best) * scale2)
        w_new = jnp.exp2((s_new - best) * scale2)
        sums = jnp.sum(w_cache, axis=0, keepdims=True) + jnp.sum(w_new, axis=0, keepdims=True)
        new_v = jnp.concatenate(
            [
                jnp.roll(
                    inbox[source + b, drows : drows + 2 * fresh, :].astype(jnp.float32),
                    -fresh,
                    axis=0,
                )
                for b in range(pairs)
            ],
            axis=0,
        ).astype(jnp.bfloat16)
        turned = w_cache.T.astype(jnp.bfloat16)
        mixed = jnp.concatenate(
            [
                jnp.dot(
                    turned[r * per : (r + 1) * per],
                    cv[start + r],
                    preferred_element_type=jnp.float32,
                )
                for r in range(own)
            ],
            axis=0,
        ).T + lax.dot_general(
            new_v,
            w_new.astype(jnp.bfloat16),
            (((0,), (0,)), ((), ())),
            preferred_element_type=jnp.float32,
        )
        mixed = jnp.concatenate([mixed, jnp.broadcast_to(sums, (ONES, 128))], axis=0)
        acc[t, :, lanes] = acc[t, :, lanes] * jnp.exp2((before - best) * scale2) + mixed
        top[t, :, lanes] = best

    for t in range(dtiles):
        lone(i, ptiles + t, first=True)
    tiles = ptiles + dtiles

    def work(s, hook=None):
        z_right, z_left = mine(s), theirs(s)
        for cc in range(2):
            for hh in range(2):
                side_wait(s, cc, hh)
        low_right = jnp.where(z_right < i, 0, ptiles)
        low_left = jnp.where(z_left < i, 0, ptiles)
        turn = tiles - low_right

        def item(e):
            rightward = e < turn
            z = jnp.where(rightward, z_right, z_left)
            t = jnp.where(rightward, low_right + e, low_left + e - turn)
            return z, t

        stream(turn + tiles - low_left, item, hook=hook)

    relay(jnp.int32(2), 0)
    work(jnp.int32(1), lambda: relay(jnp.int32(2), 1))
    for load in loads[6:]:
        load.wait()
    private_groups = dtiles * TILE // 128

    def step(s, _):
        relay(s, 0)
        for group in range(private_groups):
            pl.when(s == 3 + group)(functools.partial(private, group))
        work(s - 1, lambda: relay(s, 1))
        return 0

    lax.fori_loop(3, half, step, 0)

    work(jnp.int32(half - 1))
    for cc in range(2):
        landed(half, cc, c)
        side(half, cc, c).start()
    for cc in range(2):
        side_wait(half, cc, 1 - c)
    z = lax.rem(i + half, n)
    for t in range(dtiles):
        lone(z, ptiles + t)

    depth = acc.shape[1] - ONES
    for t in range(dtiles):
        total = acc[ptiles + t, depth : depth + 1, :]
        rows = (acc[ptiles + t, :depth, :] / total).T.astype(jnp.bfloat16)
        outbox[t * srcs : (t + 1) * srcs] = rows.reshape(srcs, drows, -1)
    for j in range(1, peers):
        outward(j).start()
    back[tp] = outbox[tp]

    @pl.when(z < i)
    def _():
        stream(jnp.int32(ptiles), lambda e: (z, e))

    def finish(t, _):
        total = acc[t, depth : depth + 1, :]
        rows = (acc[t, :depth, :] / total).T.astype(jnp.bfloat16)
        out_ref[pl.ds(pl.multiple_of(t * TILE, TILE), TILE), :] = rows
        return 0

    lax.fori_loop(0, ptiles, finish, 0)
    store = pltpu.make_async_copy(out_ref, out_hbm, load_sem.at[0])
    store.start()

    cross(h).wait_send()
    for hh in range(2):
        side(0, c, hh).wait_send()
        for cc in range(2):
            ring(0, cc, hh).wait_send()

    def drain(s, _):
        for hh in range(2):
            for cc in range(2):
                side(s, cc, hh).wait_send()

                @pl.when((s < half - 1) | (hh == c))
                def _():
                    ring(s, cc, hh).wait_send()

        return 0

    lax.fori_loop(1, half, drain, 0)
    for cc in range(2):
        side(half, cc, c).wait_send()
    for j in range(1, peers):
        inward(j).wait_send()
    for j in range(1, peers):
        outward_wait(j)
    rows = back[...].astype(jnp.float32).reshape(peers, (drows // groups), groups, -1)
    rows = jnp.swapaxes(rows, 0, 1).reshape((drows // groups), peers * groups, -1)
    dec_ref[...] = rows.astype(jnp.bfloat16)
    give = pltpu.make_async_copy(dec_ref, dec_hbm, load_sem.at[1])
    give.start()
    for j in range(1, peers):
        outward(j).wait_send()
    store.wait()
    give.wait()


def shards(n, peers, pq, pk, pv, dq, nk, nv, ck, cv, lens):
    rows, _, mine, size = pq.shape
    width = pk.shape[0]
    drow, steps, heads, groups, _ = dq.shape
    own_rows, slots = ck.shape[0], ck.shape[1]
    dr = drow * steps * groups
    fr = drow * steps
    nq = rows * mine
    nd = own_rows * steps * groups
    tiles = (nq + nd) // TILE
    half = n // 2
    bf = jnp.bfloat16
    dma = pltpu.SemaphoreType.DMA
    hbm = pl.BlockSpec(memory_space=pl.ANY)
    out, dec = pl.pallas_call(
        functools.partial(
            kernel, n, peers, slots, steps, groups, size**-0.5 * math.log2(math.e)
        ),
        out_shape=(
            jax.ShapeDtypeStruct((nq, size), bf),
            jax.ShapeDtypeStruct((fr, heads * groups, size), bf),
        ),
        in_specs=[hbm] * 8 + [pl.BlockSpec(memory_space=pltpu.SMEM)],
        out_specs=(hbm, hbm),
        scratch_shapes=[
            pltpu.VMEM((n, 2, 2, 2, width, size), bf),
            pltpu.VMEM((tiles, size, TILE), bf),
            pltpu.VMEM((tiles, size + ONES, TILE), jnp.float32),
            pltpu.VMEM((tiles, 1, TILE), jnp.float32),
            pltpu.VMEM((peers, dr + 2 * fr, size), bf),
            pltpu.VMEM((peers, dr, size), bf),
            pltpu.VMEM((peers, dr, size), bf),
            pltpu.VMEM((own_rows, slots, size), bf),
            pltpu.VMEM((own_rows, slots, size), bf),
            pltpu.VMEM((nq, size), bf),
            pltpu.VMEM((width, size), bf),
            pltpu.VMEM((width, size), bf),
            pltpu.VMEM((fr, heads, groups, size), bf),
            pltpu.VMEM((fr, heads, size), bf),
            pltpu.VMEM((fr, heads, size), bf),
            pltpu.VMEM((peers, dr + 2 * fr, size), bf),
            pltpu.VMEM((4 * width, TILE), jnp.float32),
            pltpu.VMEM((4 * width, TILE), jnp.float32),
            pltpu.VMEM((1, TILE), jnp.float32),
            pltpu.VMEM((1, TILE), jnp.float32),
            pltpu.VMEM((nq, size), bf),
            pltpu.VMEM((fr, heads * groups, size), bf),
            dma((half + 1, 2, 2)),
            dma((half + 1, 2, 2)),
            dma((half + 1, 2, 2)),
            dma((half + 1, 2, 2)),
            dma((1,)),
            dma((1,)),
            dma((peers,)),
            dma((peers,)),
            dma((peers,)),
            dma((peers,)),
            dma((8,)),
        ],
        compiler_params=pltpu.CompilerParams(
            collective_id=0, has_side_effects=True, vmem_limit_bytes=60 * 1024 * 1024
        ),
        cost_estimate=pl.CostEstimate(
            flops=4 * (nq + nd) * n * 4 * width * size,
            bytes_accessed=8 * 1024 * 1024,
            transcendentals=(nq + nd) * n * 4 * width,
        ),
        name="shared_prompt_attention",
    )(
        pq.reshape(nq, size),
        pk.reshape(width, size),
        pv.reshape(width, size),
        dq.reshape(fr, heads, groups, size),
        nk.reshape(fr, heads, size),
        nv.reshape(fr, heads, size),
        ck.reshape(own_rows, slots, size),
        cv.reshape(own_rows, slots, size),
        lens,
    )
    return out.reshape(pq.shape), dec.reshape(dq.shape)


def solution(mesh):
    return jax.shard_map(
        functools.partial(shards, mesh.shape["ctx"], mesh.shape["tp"]),
        mesh=mesh,
        in_specs=(
            P("ctx", "tp", "sec", None),
            P(("ctx", "sec"), "tp", None),
            P(("ctx", "sec"), "tp", None),
            P(("ctx", "sec", "tp"), None, None, None, None),
            P(("ctx", "sec", "tp"), None, None, None),
            P(("ctx", "sec", "tp"), None, None, None),
            P(("ctx", "sec"), None, "tp", None),
            P(("ctx", "sec"), None, "tp", None),
            P(("ctx", "sec")),
        ),
        out_specs=(P("ctx", "tp", "sec", None), P(("ctx", "sec", "tp"), None, None, None, None)),
        check_vma=False,
    )
```

```python
import functools
import math

import jax
import jax.numpy as jnp
from jax import lax
from jax.experimental import pallas as pl
from jax.experimental.pallas import tpu as pltpu
from jax.sharding import PartitionSpec as P

NEG = -1e30
MESH = pl.DeviceIdType.MESH
TILE = 512
ONES = 16


def kernel(
    n, peers, slots, steps, groups, scale2,
    pq_hbm, k_hbm, v_hbm, dq_hbm, nk_hbm, nv_hbm, ck_hbm, cv_hbm, lens_ref,
    out_hbm, dec_hbm,
    kv, qt, acc, top, inbox, outbox, back, ck, cv,
    pq_ref, k_ref, v_ref, dq, nk, nv, pack_ref, score_a, score_b, high_a, high_b,
    out_ref,
    ring_send, ring_recv, sib_send, sib_recv, y_send, y_recv,
    in_send, in_recv, out_send, out_recv, load_sem,
):
    i = lax.axis_index("ctx")
    sec = lax.axis_index("sec")
    tp = lax.axis_index("tp")
    half = n // 2
    h, c = sec // 2, lax.rem(sec, 2)
    right = lax.rem(i + 1, n)
    left = lax.rem(i + n - 1, n)
    to_right, to_left = (right, sec, tp), (left, sec, tp)
    sibling = (i, h * 2 + 1 - c, tp)
    across = (i, (1 - h) * 2 + c, tp)
    width = k_ref.shape[0]
    block = 4 * width
    ptiles = pq_ref.shape[0] // TILE
    dtiles = qt.shape[0] - ptiles
    drows = outbox.shape[1]
    srcs = TILE // drows

    barrier = pltpu.get_barrier_semaphore()
    for device in (to_right, to_left, sibling, across):
        pl.semaphore_signal(barrier, inc=1, device_id=device, device_id_type=MESH)
    for j in range(1, peers):
        device = (i, sec, lax.rem(tp + j, peers))
        pl.semaphore_signal(barrier, inc=1, device_id=device, device_id_type=MESH)

    sources = (k_hbm, v_hbm, dq_hbm, nk_hbm, nv_hbm, pq_hbm, ck_hbm, cv_hbm)
    targets = (k_ref, v_ref, dq, nk, nv, pq_ref, ck, cv)
    loads = [
        pltpu.make_async_copy(source, target, load_sem.at[at])
        for at, (source, target) in enumerate(zip(sources, targets))
    ]
    for load in loads:
        load.start()
    loads[0].wait()
    loads[1].wait()
    kv[i, h, c, 0] = k_ref[...]
    kv[i, h, c, 1] = v_ref[...].astype(jnp.float32).T.astype(jnp.bfloat16)
    pl.semaphore_wait(barrier, 3 + peers)

    sign = 1 - 2 * c
    onward = (jnp.where(c == 0, right, left), sec, tp)

    def mine(s):
        return lax.rem(i + n - s * sign, n)

    def theirs(s):
        return lax.rem(i + n + s * sign, n)

    def slot_of(cc):
        return 0 if cc is None else cc

    def part(z, cc, hh):
        return kv.at[z, hh] if cc is None else kv.at[z, hh, cc]

    def ring(s, cc, hh):
        return pltpu.make_async_remote_copy(
            src_ref=part(mine(s), cc, hh),
            dst_ref=part(mine(s), cc, hh),
            send_sem=ring_send.at[s, slot_of(cc), hh],
            recv_sem=ring_recv.at[s + 1, slot_of(cc), hh],
            device_id=onward,
            device_id_type=MESH,
        )

    def side(s, cc, hh, z=None):
        z = mine(s) if z is None else z
        return pltpu.make_async_remote_copy(
            src_ref=part(z, cc, hh),
            dst_ref=part(z, cc, hh),
            send_sem=sib_send.at[s, slot_of(cc), hh],
            recv_sem=sib_recv.at[s, slot_of(cc), hh],
            device_id=sibling,
            device_id_type=MESH,
        )

    def side_wait(s, cc, hh):
        side(s, cc, hh, theirs(s)).wait_recv()

    def landed(s, cc, hh):
        pltpu.make_async_remote_copy(
            src_ref=part(mine(s), cc, hh),
            dst_ref=part(mine(s), cc, hh),
            send_sem=ring_send.at[s - 1, slot_of(cc), hh],
            recv_sem=ring_recv.at[s, slot_of(cc), hh],
            device_id=onward,
            device_id_type=MESH,
        ).wait_recv()

    def cross(hh):
        return pltpu.make_async_remote_copy(
            src_ref=kv.at[i, hh, c],
            dst_ref=kv.at[i, hh, c],
            send_sem=y_send.at[0],
            recv_sem=y_recv.at[0],
            device_id=across,
            device_id_type=MESH,
        )

    def inward(j):
        to = lax.rem(tp + j, peers)
        return pltpu.make_async_remote_copy(
            src_ref=pack_ref.at[to],
            dst_ref=inbox.at[tp],
            send_sem=in_send.at[j],
            recv_sem=in_recv.at[j],
            device_id=(i, sec, to),
            device_id_type=MESH,
        )

    def inward_wait(j):
        source = lax.rem(tp + peers - j, peers)
        pltpu.make_async_remote_copy(
            src_ref=pack_ref.at[source],
            dst_ref=inbox.at[source],
            send_sem=in_send.at[j],
            recv_sem=in_recv.at[j],
            device_id=(i, sec, source),
            device_id_type=MESH,
        ).wait_recv()

    def outward(j):
        to = lax.rem(tp + j, peers)
        return pltpu.make_async_remote_copy(
            src_ref=outbox.at[to],
            dst_ref=back.at[tp],
            send_sem=out_send.at[j],
            recv_sem=out_recv.at[j],
            device_id=(i, sec, to),
            device_id_type=MESH,
        )

    def outward_wait(j):
        source = lax.rem(tp + peers - j, peers)
        pltpu.make_async_remote_copy(
            src_ref=outbox.at[source],
            dst_ref=back.at[source],
            send_sem=out_send.at[j],
            recv_sem=out_recv.at[j],
            device_id=(i, sec, source),
            device_id_type=MESH,
        ).wait_recv()

    ring(0, c, h).start()
    cross(h).start()
    side(0, c, h).start()
    for at in range(2, 5):
        loads[at].wait()
    queries = jnp.swapaxes(dq[...].astype(jnp.float32), 0, 1).reshape(peers, drows, -1)
    pack_ref[:, :drows, :] = queries.astype(jnp.bfloat16)
    pack_ref[:, drows:, :] = jnp.concatenate(
        [jnp.swapaxes(new[...].astype(jnp.float32), 0, 1) for new in (nk, nv)], axis=1
    ).astype(jnp.bfloat16)
    for j in range(1, peers):
        inward(j).start()
    inbox[tp] = pack_ref[tp]

    def turn_queries(rows):
        return rows.astype(jnp.float32).T.astype(jnp.bfloat16)

    def prepare(t, _):
        qt[t] = turn_queries(pq_ref[pl.ds(pl.multiple_of(t * TILE, TILE), TILE), :])
        return 0

    side_wait(0, 1 - c, h)
    ring(0, 1 - c, h).start()
    cross(1 - h).wait_recv()
    ring(0, c, 1 - h).start()
    side(0, c, 1 - h).start()
    side_wait(0, 1 - c, 1 - h)
    ring(0, 1 - c, 1 - h).start()
    loads[5].wait()
    lax.fori_loop(0, ptiles, prepare, 0)

    def advance(now, later, scores, high, scores_next, high_next, first, mask):
        z, t = now
        best = high[...]
        if not first:
            before = top[t]
            best = jnp.maximum(before, best)
        if later is not None:
            ahead(*later, scores_next, high_next, mask)
        weights = jnp.exp2((scores[...] - best) * scale2).astype(jnp.bfloat16)
        values = jnp.concatenate([kv[z, b, a, 1] for b in range(2) for a in range(2)], axis=1)
        values = jnp.concatenate([values, jnp.ones((ONES, block), jnp.bfloat16)], axis=0)
        mixed = jnp.dot(values, weights, preferred_element_type=jnp.float32)
        if not first:
            mixed = acc[t] * jnp.exp2((before - best) * scale2) + mixed
        acc[t] = mixed
        top[t] = best

    def ahead(z, t, scores, high, mask=None):
        keys = kv[z, :, :, 0].reshape(block, k_ref.shape[1])
        found = jnp.dot(keys, qt[t], preferred_element_type=jnp.float32)
        if mask is not None:
            found = jnp.where(mask(t), found, NEG)
        scores[...] = found
        high[...] = jnp.max(found, axis=0, keepdims=True)

    def lone(z, t, first=False):
        ahead(z, t, score_a, high_a)
        advance((z, t), None, score_a, high_a, None, None, first, None)

    def stream(count, item, first=False, mask=None, hook=None):
        def one(u, _):
            now, second = item(2 * u), item(2 * u + 1)
            later = item(jnp.minimum(2 * u + 2, count - 1))
            if hook is not None:
                pl.when(u == count // 4)(hook)
            advance(now, second, score_a, high_a, score_b, high_b, first, mask)
            advance(second, later, score_b, high_b, score_a, high_a, first, mask)
            return 0

        ahead(*item(0), score_a, high_a, mask)
        lax.fori_loop(0, count // 2, one, 0)

    def causal(t):
        position = lax.broadcasted_iota(jnp.int32, (block, TILE), 0)
        query = (t * TILE + lax.broadcasted_iota(jnp.int32, (block, TILE), 1)) // 2
        return position <= query

    def relay(s, order, apart=False):
        hh = h if order == 0 else 1 - h
        for cc in (c, 1 - c) if apart else (None,):
            landed(s, cc, hh)

        @pl.when((s < half - 1) | (hh == c))
        def _():
            ring(s, None, hh).start()

        side(s, None, hh).start()

    relay(jnp.int32(1), 0, True)
    stream(
        jnp.int32(ptiles), lambda e: (i, e), first=True, mask=causal,
        hook=lambda: relay(jnp.int32(1), 1, True),
    )

    for j in range(1, peers):
        inward_wait(j)
    for t in range(dtiles):
        rows = inbox[t * srcs : (t + 1) * srcs, :drows, :].reshape(TILE, -1)
        qt[ptiles + t] = turn_queries(rows)

    per = steps * groups
    own = 128 // per
    pairs = 128 // drows
    fresh = (inbox.shape[1] - drows) // 2

    def private(group):
        t, lanes = ptiles + group * 128 // TILE, pl.ds(group * 128 % TILE, 128)
        start = group * own
        queries = qt[t, :, lanes]
        lane_row = lax.broadcasted_iota(jnp.int32, (slots, 128), 1) // per
        limit = jnp.full((slots, 128), lens_ref[start], jnp.int32)
        s_cache = jnp.dot(ck[start], queries, preferred_element_type=jnp.float32)
        for r in range(1, own):
            found = jnp.dot(ck[start + r], queries, preferred_element_type=jnp.float32)
            s_cache = jnp.where(lane_row == r, found, s_cache)
            limit = jnp.where(lane_row == r, lens_ref[start + r], limit)
        slot = lax.broadcasted_iota(jnp.int32, (slots, 128), 0)
        s_cache = jnp.where(slot < limit, s_cache, NEG)
        source = group * pairs
        new_k = jnp.concatenate(
            [inbox[source + b, drows : drows + 2 * fresh, :] for b in range(pairs)], axis=0
        )
        s_new = jnp.dot(new_k, queries, preferred_element_type=jnp.float32)
        shape = (pairs * 2 * fresh, 128)
        key_id = lax.broadcasted_iota(jnp.int32, shape, 0)
        lane = lax.broadcasted_iota(jnp.int32, shape, 1)
        in_pair = lax.rem(key_id, 2 * fresh)
        key_row = key_id // (2 * fresh) * (fresh // steps) + in_pair // steps
        key_step = lax.rem(in_pair, steps)
        ok = (
            (in_pair < fresh)
            & (key_row == lane // per)
            & (key_step <= lax.rem(lane, per) // groups)
        )
        s_new = jnp.where(ok, s_new, NEG)
        before = top[t, :, lanes]
        best = jnp.maximum(
            jnp.max(s_cache, axis=0, keepdims=True), jnp.max(s_new, axis=0, keepdims=True)
        )
        best = jnp.maximum(before, best)
        w_cache = jnp.exp2((s_cache - best) * scale2)
        w_new = jnp.exp2((s_new - best) * scale2)
        sums = jnp.sum(w_cache, axis=0, keepdims=True) + jnp.sum(w_new, axis=0, keepdims=True)
        new_v = jnp.concatenate(
            [
                jnp.roll(
                    inbox[source + b, drows : drows + 2 * fresh, :].astype(jnp.float32),
                    -fresh,
                    axis=0,
                )
                for b in range(pairs)
            ],
            axis=0,
        ).astype(jnp.bfloat16)
        turned = w_cache.T.astype(jnp.bfloat16)
        mixed = jnp.concatenate(
            [
                jnp.dot(
                    turned[r * per : (r + 1) * per],
                    cv[start + r],
                    preferred_element_type=jnp.float32,
                )
                for r in range(own)
            ],
            axis=0,
        ).T + lax.dot_general(
            new_v,
            w_new.astype(jnp.bfloat16),
            (((0,), (0,)), ((), ())),
            preferred_element_type=jnp.float32,
        )
        mixed = jnp.concatenate([mixed, jnp.broadcast_to(sums, (ONES, 128))], axis=0)
        acc[t, :, lanes] = acc[t, :, lanes] * jnp.exp2((before - best) * scale2) + mixed
        top[t, :, lanes] = best

    for t in range(dtiles):
        lone(i, ptiles + t, first=True)
    tiles = ptiles + dtiles

    def work(s, hook=None):
        z_right, z_left = mine(s), theirs(s)
        for hh in range(2):
            side_wait(s, None, hh)
        low_right = jnp.where(z_right < i, 0, ptiles)
        low_left = jnp.where(z_left < i, 0, ptiles)
        turn = tiles - low_right

        def item(e):
            rightward = e < turn
            z = jnp.where(rightward, z_right, z_left)
            t = jnp.where(rightward, low_right + e, low_left + e - turn)
            return z, t

        stream(turn + tiles - low_left, item, hook=hook)

    relay(jnp.int32(2), 0)
    work(jnp.int32(1), lambda: relay(jnp.int32(2), 1))
    for load in loads[6:]:
        load.wait()
    private_groups = dtiles * TILE // 128

    def step(s, _):
        relay(s, 0)
        for group in range(private_groups):
            pl.when(s == 3 + group)(functools.partial(private, group))
        work(s - 1, lambda: relay(s, 1))
        return 0

    lax.fori_loop(3, half, step, 0)

    work(jnp.int32(half - 1))
    landed(half, None, c)
    side(half, None, c).start()
    side_wait(half, None, 1 - c)
    z = lax.rem(i + half, n)
    for t in range(dtiles):
        lone(z, ptiles + t)

    depth = acc.shape[1] - ONES
    for t in range(dtiles):
        total = acc[ptiles + t, depth : depth + 1, :]
        rows = (acc[ptiles + t, :depth, :] / total).T.astype(jnp.bfloat16)
        outbox[t * srcs : (t + 1) * srcs] = rows.reshape(srcs, drows, -1)
    for j in range(1, peers):
        outward(j).start()
    back[tp] = outbox[tp]

    @pl.when(z < i)
    def _():
        stream(jnp.int32(ptiles), lambda e: (z, e))

    def finish(t, _):
        total = acc[t, depth : depth + 1, :]
        rows = (acc[t, :depth, :] / total).T.astype(jnp.bfloat16)
        out_ref[pl.ds(pl.multiple_of(t * TILE, TILE), TILE), :] = rows
        return 0

    lax.fori_loop(0, ptiles, finish, 0)
    store = pltpu.make_async_copy(out_ref, out_hbm, load_sem.at[0])
    store.start()

    cross(h).wait_send()
    for hh in range(2):
        side(0, c, hh).wait_send()
        for cc in range(2):
            ring(0, cc, hh).wait_send()

    def drain(s, _):
        for hh in range(2):
            side(s, None, hh).wait_send()

            @pl.when((s < half - 1) | (hh == c))
            def _():
                ring(s, None, hh).wait_send()

        return 0

    lax.fori_loop(1, half, drain, 0)
    side(half, None, c).wait_send()
    for j in range(1, peers):
        inward(j).wait_send()
    for j in range(1, peers):
        outward_wait(j)
    give = pltpu.make_async_copy(back, dec_hbm, load_sem.at[1])
    give.start()
    for j in range(1, peers):
        outward(j).wait_send()
    store.wait()
    give.wait()


def shards(n, peers, pq, pk, pv, dq, nk, nv, ck, cv, lens):
    rows, _, mine, size = pq.shape
    width = pk.shape[0]
    drow, steps, heads, groups, _ = dq.shape
    own_rows, slots = ck.shape[0], ck.shape[1]
    dr = drow * steps * groups
    fr = drow * steps
    nq = rows * mine
    nd = own_rows * steps * groups
    tiles = (nq + nd) // TILE
    half = n // 2
    bf = jnp.bfloat16
    dma = pltpu.SemaphoreType.DMA
    hbm = pl.BlockSpec(memory_space=pl.ANY)
    out, dec = pl.pallas_call(
        functools.partial(
            kernel, n, peers, slots, steps, groups, size**-0.5 * math.log2(math.e)
        ),
        out_shape=(
            jax.ShapeDtypeStruct((nq, size), bf),
            jax.ShapeDtypeStruct((heads, dr, size), bf),
        ),
        in_specs=[hbm] * 8 + [pl.BlockSpec(memory_space=pltpu.SMEM)],
        out_specs=(hbm, hbm),
        scratch_shapes=[
            pltpu.VMEM((n, 2, 2, 2, width, size), bf),
            pltpu.VMEM((tiles, size, TILE), bf),
            pltpu.VMEM((tiles, size + ONES, TILE), jnp.float32),
            pltpu.VMEM((tiles, 1, TILE), jnp.float32),
            pltpu.VMEM((peers, dr + 2 * fr, size), bf),
            pltpu.VMEM((peers, dr, size), bf),
            pltpu.VMEM((peers, dr, size), bf),
            pltpu.VMEM((own_rows, slots, size), bf),
            pltpu.VMEM((own_rows, slots, size), bf),
            pltpu.VMEM((nq, size), bf),
            pltpu.VMEM((width, size), bf),
            pltpu.VMEM((width, size), bf),
            pltpu.VMEM((fr, heads, groups, size), bf),
            pltpu.VMEM((fr, heads, size), bf),
            pltpu.VMEM((fr, heads, size), bf),
            pltpu.VMEM((peers, dr + 2 * fr, size), bf),
            pltpu.VMEM((4 * width, TILE), jnp.float32),
            pltpu.VMEM((4 * width, TILE), jnp.float32),
            pltpu.VMEM((1, TILE), jnp.float32),
            pltpu.VMEM((1, TILE), jnp.float32),
            pltpu.VMEM((nq, size), bf),
            dma((half + 1, 2, 2)),
            dma((half + 1, 2, 2)),
            dma((half + 1, 2, 2)),
            dma((half + 1, 2, 2)),
            dma((1,)),
            dma((1,)),
            dma((peers,)),
            dma((peers,)),
            dma((peers,)),
            dma((peers,)),
            dma((8,)),
        ],
        compiler_params=pltpu.CompilerParams(
            collective_id=0, has_side_effects=True, vmem_limit_bytes=60 * 1024 * 1024
        ),
        cost_estimate=pl.CostEstimate(
            flops=4 * (nq + nd) * n * 4 * width * size,
            bytes_accessed=8 * 1024 * 1024,
            transcendentals=(nq + nd) * n * 4 * width,
        ),
        name="shared_prompt_attention",
    )(
        pq.reshape(nq, size),
        pk.reshape(width, size),
        pv.reshape(width, size),
        dq.reshape(fr, heads, groups, size),
        nk.reshape(fr, heads, size),
        nv.reshape(fr, heads, size),
        ck.reshape(own_rows, slots, size),
        cv.reshape(own_rows, slots, size),
        lens,
    )
    decoded = jnp.moveaxis(dec.reshape(heads, drow, steps, groups, size), 0, 2)
    return out.reshape(pq.shape), decoded


def solution(mesh):
    return jax.shard_map(
        functools.partial(shards, mesh.shape["ctx"], mesh.shape["tp"]),
        mesh=mesh,
        in_specs=(
            P("ctx", "tp", "sec", None),
            P(("ctx", "sec"), "tp", None),
            P(("ctx", "sec"), "tp", None),
            P(("ctx", "sec", "tp"), None, None, None, None),
            P(("ctx", "sec", "tp"), None, None, None),
            P(("ctx", "sec", "tp"), None, None, None),
            P(("ctx", "sec"), None, "tp", None),
            P(("ctx", "sec"), None, "tp", None),
            P(("ctx", "sec")),
        ),
        out_specs=(P("ctx", "tp", "sec", None), P(("ctx", "sec", "tp"), None, None, None, None)),
        check_vma=False,
    )
```

```python
import functools
import math

import jax
import jax.numpy as jnp
from jax import lax
from jax.experimental import pallas as pl
from jax.experimental.pallas import tpu as pltpu
from jax.sharding import PartitionSpec as P

NEG = -1e30
MESH = pl.DeviceIdType.MESH
TILE = 512
ONES = 16


def kernel(
    n, peers, slots, steps, groups, scale2,
    pq_hbm, k_hbm, v_hbm, dq_hbm, nk_hbm, nv_hbm, ck_hbm, cv_hbm, lens_ref,
    out_hbm, dec_hbm,
    kv, qt, acc, top, inbox, outbox, back, ck, cv,
    pq_ref, k_ref, v_ref, dq, nk, nv, pack_ref, score_a, score_b, high_a, high_b,
    out_ref,
    ring_send, ring_recv, sib_send, sib_recv, y_send, y_recv,
    in_send, in_recv, out_send, out_recv, load_sem,
):
    i = lax.axis_index("ctx")
    sec = lax.axis_index("sec")
    tp = lax.axis_index("tp")
    half = n // 2
    h, c = sec // 2, lax.rem(sec, 2)
    right = lax.rem(i + 1, n)
    left = lax.rem(i + n - 1, n)
    to_right, to_left = (right, sec, tp), (left, sec, tp)
    sibling = (i, h * 2 + 1 - c, tp)
    across = (i, (1 - h) * 2 + c, tp)
    width = k_ref.shape[0]
    block = 4 * width
    ptiles = pq_ref.shape[0] // TILE
    dtiles = qt.shape[0] - ptiles
    drows = outbox.shape[1]
    srcs = TILE // drows

    barrier = pltpu.get_barrier_semaphore()
    for device in (to_right, to_left, sibling, across):
        pl.semaphore_signal(barrier, inc=1, device_id=device, device_id_type=MESH)
    for j in range(1, peers):
        device = (i, sec, lax.rem(tp + j, peers))
        pl.semaphore_signal(barrier, inc=1, device_id=device, device_id_type=MESH)

    sources = (k_hbm, v_hbm, dq_hbm, nk_hbm, nv_hbm, pq_hbm, ck_hbm, cv_hbm)
    targets = (k_ref, v_ref, dq, nk, nv, pq_ref, ck, cv)
    loads = [
        pltpu.make_async_copy(source, target, load_sem.at[at])
        for at, (source, target) in enumerate(zip(sources, targets))
    ]
    for load in loads:
        load.start()
    loads[0].wait()
    loads[1].wait()
    kv[i, c, h, 0] = k_ref[...]
    kv[i, c, h, 1] = v_ref[...].astype(jnp.float32).T.astype(jnp.bfloat16)
    pl.semaphore_wait(barrier, 3 + peers)

    sign = 1 - 2 * c
    onward = (jnp.where(c == 0, right, left), sec, tp)

    def mine(s):
        return lax.rem(i + n - s * sign, n)

    def theirs(s):
        return lax.rem(i + n + s * sign, n)

    def ring(s, cc, hh, w):
        return pltpu.make_async_remote_copy(
            src_ref=kv.at[mine(s), cc, hh, w],
            dst_ref=kv.at[mine(s), cc, hh, w],
            send_sem=ring_send.at[s, cc, hh, w],
            recv_sem=ring_recv.at[s + 1, cc, hh, w],
            device_id=onward,
            device_id_type=MESH,
        )

    def launch(s, cc, hh):
        for w in range(2):
            ring(s, cc, hh, w).start()

    def side(s, cc, hh, z=None):
        z = mine(s) if z is None else z
        return pltpu.make_async_remote_copy(
            src_ref=kv.at[z, cc, hh],
            dst_ref=kv.at[z, cc, hh],
            send_sem=sib_send.at[s, cc, hh],
            recv_sem=sib_recv.at[s, cc, hh],
            device_id=sibling,
            device_id_type=MESH,
        )

    def side_wait(s, cc, hh):
        side(s, cc, hh, theirs(s)).wait_recv()

    def landed(s, cc, hh, w):
        pltpu.make_async_remote_copy(
            src_ref=kv.at[mine(s), cc, hh, w],
            dst_ref=kv.at[mine(s), cc, hh, w],
            send_sem=ring_send.at[s - 1, cc, hh, w],
            recv_sem=ring_recv.at[s, cc, hh, w],
            device_id=onward,
            device_id_type=MESH,
        ).wait_recv()

    def cross(hh):
        return pltpu.make_async_remote_copy(
            src_ref=kv.at[i, c, hh],
            dst_ref=kv.at[i, c, hh],
            send_sem=y_send.at[0],
            recv_sem=y_recv.at[0],
            device_id=across,
            device_id_type=MESH,
        )

    def inward(j):
        to = lax.rem(tp + j, peers)
        return pltpu.make_async_remote_copy(
            src_ref=pack_ref.at[to],
            dst_ref=inbox.at[tp],
            send_sem=in_send.at[j],
            recv_sem=in_recv.at[j],
            device_id=(i, sec, to),
            device_id_type=MESH,
        )

    def inward_wait(j):
        source = lax.rem(tp + peers - j, peers)
        pltpu.make_async_remote_copy(
            src_ref=pack_ref.at[source],
            dst_ref=inbox.at[source],
            send_sem=in_send.at[j],
            recv_sem=in_recv.at[j],
            device_id=(i, sec, source),
            device_id_type=MESH,
        ).wait_recv()

    def outward(j):
        to = lax.rem(tp + j, peers)
        return pltpu.make_async_remote_copy(
            src_ref=outbox.at[to],
            dst_ref=back.at[tp],
            send_sem=out_send.at[j],
            recv_sem=out_recv.at[j],
            device_id=(i, sec, to),
            device_id_type=MESH,
        )

    def outward_wait(j):
        source = lax.rem(tp + peers - j, peers)
        pltpu.make_async_remote_copy(
            src_ref=outbox.at[source],
            dst_ref=back.at[source],
            send_sem=out_send.at[j],
            recv_sem=out_recv.at[j],
            device_id=(i, sec, source),
            device_id_type=MESH,
        ).wait_recv()

    launch(0, c, h)
    cross(h).start()
    side(0, c, h).start()
    for at in range(2, 5):
        loads[at].wait()
    queries = jnp.swapaxes(dq[...].astype(jnp.float32), 0, 1).reshape(peers, drows, -1)
    pack_ref[:, :drows, :] = queries.astype(jnp.bfloat16)
    pack_ref[:, drows:, :] = jnp.concatenate(
        [jnp.swapaxes(new[...].astype(jnp.float32), 0, 1) for new in (nk, nv)], axis=1
    ).astype(jnp.bfloat16)
    for j in range(1, peers):
        inward(j).start()
    inbox[tp] = pack_ref[tp]

    def turn_queries(rows):
        return rows.astype(jnp.float32).T.astype(jnp.bfloat16)

    def prepare(t, _):
        qt[t] = turn_queries(pq_ref[pl.ds(pl.multiple_of(t * TILE, TILE), TILE), :])
        return 0

    side_wait(0, 1 - c, h)
    launch(0, 1 - c, h)
    cross(1 - h).wait_recv()
    launch(0, c, 1 - h)
    side(0, c, 1 - h).start()
    side_wait(0, 1 - c, 1 - h)
    launch(0, 1 - c, 1 - h)
    loads[5].wait()
    lax.fori_loop(0, ptiles, prepare, 0)

    def advance(now, later, scores, high, scores_next, high_next, first, mask):
        z, t = now
        best = high[...]
        if not first:
            before = top[t]
            best = jnp.maximum(before, best)
        if later is not None:
            ahead(*later, scores_next, high_next, mask)
        weights = jnp.exp2((scores[...] - best) * scale2).astype(jnp.bfloat16)
        values = jnp.concatenate([kv[z, a, b, 1] for a in range(2) for b in range(2)], axis=1)
        values = jnp.concatenate([values, jnp.ones((ONES, block), jnp.bfloat16)], axis=0)
        mixed = jnp.dot(values, weights, preferred_element_type=jnp.float32)
        if not first:
            mixed = acc[t] * jnp.exp2((before - best) * scale2) + mixed
        acc[t] = mixed
        top[t] = best

    def ahead(z, t, scores, high, mask=None):
        keys = kv[z, :, :, 0].reshape(block, k_ref.shape[1])
        found = jnp.dot(keys, qt[t], preferred_element_type=jnp.float32)
        if mask is not None:
            found = jnp.where(mask(t), found, NEG)
        scores[...] = found
        high[...] = jnp.max(found, axis=0, keepdims=True)

    def lone(z, t, first=False):
        ahead(z, t, score_a, high_a)
        advance((z, t), None, score_a, high_a, None, None, first, None)

    def stream(count, item, first=False, mask=None, hook=None):
        def one(u, _):
            now, second = item(2 * u), item(2 * u + 1)
            later = item(jnp.minimum(2 * u + 2, count - 1))
            if hook is not None:
                pl.when(u == count // 4)(hook)
            advance(now, second, score_a, high_a, score_b, high_b, first, mask)
            advance(second, later, score_b, high_b, score_a, high_a, first, mask)
            return 0

        ahead(*item(0), score_a, high_a, mask)
        lax.fori_loop(0, count // 2, one, 0)

    def causal(t):
        slot = lax.broadcasted_iota(jnp.int32, (block, TILE), 0)
        core, upper = slot // (2 * width), lax.rem(slot // width, 2)
        position = (upper * 2 + core) * width + lax.rem(slot, width)
        query = (t * TILE + lax.broadcasted_iota(jnp.int32, (block, TILE), 1)) // 2
        return position <= query

    def relay(s, order):
        hh = h if order == 0 else 1 - h
        for cc in (c, 1 - c):
            for w in range(2):
                landed(s, cc, hh, w)

                @pl.when((s < half - 1) | (hh == c))
                def _():
                    ring(s, cc, hh, w).start()

            side(s, cc, hh).start()

    relay(jnp.int32(1), 0)
    stream(
        jnp.int32(ptiles), lambda e: (i, e), first=True, mask=causal,
        hook=lambda: relay(jnp.int32(1), 1),
    )

    for j in range(1, peers):
        inward_wait(j)
    for t in range(dtiles):
        rows = inbox[t * srcs : (t + 1) * srcs, :drows, :].reshape(TILE, -1)
        qt[ptiles + t] = turn_queries(rows)

    per = steps * groups
    own = 128 // per
    pairs = 128 // drows
    fresh = (inbox.shape[1] - drows) // 2

    def private(group):
        t, lanes = ptiles + group * 128 // TILE, pl.ds(group * 128 % TILE, 128)
        start = group * own
        queries = qt[t, :, lanes]
        lane_row = lax.broadcasted_iota(jnp.int32, (slots, 128), 1) // per
        limit = jnp.full((slots, 128), lens_ref[start], jnp.int32)
        s_cache = jnp.dot(ck[start], queries, preferred_element_type=jnp.float32)
        for r in range(1, own):
            found = jnp.dot(ck[start + r], queries, preferred_element_type=jnp.float32)
            s_cache = jnp.where(lane_row == r, found, s_cache)
            limit = jnp.where(lane_row == r, lens_ref[start + r], limit)
        slot = lax.broadcasted_iota(jnp.int32, (slots, 128), 0)
        s_cache = jnp.where(slot < limit, s_cache, NEG)
        source = group * pairs
        new_k = jnp.concatenate(
            [inbox[source + b, drows : drows + 2 * fresh, :] for b in range(pairs)], axis=0
        )
        s_new = jnp.dot(new_k, queries, preferred_element_type=jnp.float32)
        shape = (pairs * 2 * fresh, 128)
        key_id = lax.broadcasted_iota(jnp.int32, shape, 0)
        lane = lax.broadcasted_iota(jnp.int32, shape, 1)
        in_pair = lax.rem(key_id, 2 * fresh)
        key_row = key_id // (2 * fresh) * (fresh // steps) + in_pair // steps
        key_step = lax.rem(in_pair, steps)
        ok = (
            (in_pair < fresh)
            & (key_row == lane // per)
            & (key_step <= lax.rem(lane, per) // groups)
        )
        s_new = jnp.where(ok, s_new, NEG)
        before = top[t, :, lanes]
        best = jnp.maximum(
            jnp.max(s_cache, axis=0, keepdims=True), jnp.max(s_new, axis=0, keepdims=True)
        )
        best = jnp.maximum(before, best)
        w_cache = jnp.exp2((s_cache - best) * scale2)
        w_new = jnp.exp2((s_new - best) * scale2)
        sums = jnp.sum(w_cache, axis=0, keepdims=True) + jnp.sum(w_new, axis=0, keepdims=True)
        new_v = jnp.concatenate(
            [
                jnp.roll(
                    inbox[source + b, drows : drows + 2 * fresh, :].astype(jnp.float32),
                    -fresh,
                    axis=0,
                )
                for b in range(pairs)
            ],
            axis=0,
        ).astype(jnp.bfloat16)
        turned = w_cache.T.astype(jnp.bfloat16)
        mixed = jnp.concatenate(
            [
                jnp.dot(
                    turned[r * per : (r + 1) * per],
                    cv[start + r],
                    preferred_element_type=jnp.float32,
                )
                for r in range(own)
            ],
            axis=0,
        ).T + lax.dot_general(
            new_v,
            w_new.astype(jnp.bfloat16),
            (((0,), (0,)), ((), ())),
            preferred_element_type=jnp.float32,
        )
        mixed = jnp.concatenate([mixed, jnp.broadcast_to(sums, (ONES, 128))], axis=0)
        acc[t, :, lanes] = acc[t, :, lanes] * jnp.exp2((before - best) * scale2) + mixed
        top[t, :, lanes] = best

    for t in range(dtiles):
        lone(i, ptiles + t, first=True)
    tiles = ptiles + dtiles

    def work(s, hook=None):
        z_right, z_left = mine(s), theirs(s)
        for cc in range(2):
            for hh in range(2):
                side_wait(s, cc, hh)
        low_right = jnp.where(z_right < i, 0, ptiles)
        low_left = jnp.where(z_left < i, 0, ptiles)
        turn = tiles - low_right

        def item(e):
            rightward = e < turn
            z = jnp.where(rightward, z_right, z_left)
            t = jnp.where(rightward, low_right + e, low_left + e - turn)
            return z, t

        stream(turn + tiles - low_left, item, hook=hook)

    relay(jnp.int32(2), 0)
    work(jnp.int32(1), lambda: relay(jnp.int32(2), 1))
    for load in loads[6:]:
        load.wait()
    private_groups = dtiles * TILE // 128

    def step(s, _):
        relay(s, 0)
        for group in range(private_groups):
            pl.when(s == 3 + group)(functools.partial(private, group))
        work(s - 1, lambda: relay(s, 1))
        return 0

    lax.fori_loop(3, half, step, 0)

    work(jnp.int32(half - 1))
    for cc in range(2):
        for w in range(2):
            landed(half, cc, c, w)
        side(half, cc, c).start()
    for cc in range(2):
        side_wait(half, cc, 1 - c)
    z = lax.rem(i + half, n)
    for t in range(dtiles):
        lone(z, ptiles + t)

    depth = acc.shape[1] - ONES
    for t in range(dtiles):
        total = acc[ptiles + t, depth : depth + 1, :]
        rows = (acc[ptiles + t, :depth, :] / total).T.astype(jnp.bfloat16)
        outbox[t * srcs : (t + 1) * srcs] = rows.reshape(srcs, drows, -1)
    for j in range(1, peers):
        outward(j).start()
    back[tp] = outbox[tp]

    @pl.when(z < i)
    def _():
        stream(jnp.int32(ptiles), lambda e: (z, e))

    def finish(t, _):
        total = acc[t, depth : depth + 1, :]
        rows = (acc[t, :depth, :] / total).T.astype(jnp.bfloat16)
        out_ref[pl.ds(pl.multiple_of(t * TILE, TILE), TILE), :] = rows
        return 0

    lax.fori_loop(0, ptiles, finish, 0)
    store = pltpu.make_async_copy(out_ref, out_hbm, load_sem.at[0])
    store.start()

    cross(h).wait_send()
    for hh in range(2):
        side(0, c, hh).wait_send()
        for cc in range(2):
            for w in range(2):
                ring(0, cc, hh, w).wait_send()

    def drain(s, _):
        for hh in range(2):
            for cc in range(2):
                side(s, cc, hh).wait_send()

                @pl.when((s < half - 1) | (hh == c))
                def _():
                    for w in range(2):
                        ring(s, cc, hh, w).wait_send()

        return 0

    lax.fori_loop(1, half, drain, 0)
    for cc in range(2):
        side(half, cc, c).wait_send()
    for j in range(1, peers):
        inward(j).wait_send()
    for j in range(1, peers):
        outward_wait(j)
    give = pltpu.make_async_copy(back, dec_hbm, load_sem.at[1])
    give.start()
    for j in range(1, peers):
        outward(j).wait_send()
    store.wait()
    give.wait()


def shards(n, peers, pq, pk, pv, dq, nk, nv, ck, cv, lens):
    rows, _, mine, size = pq.shape
    width = pk.shape[0]
    drow, steps, heads, groups, _ = dq.shape
    own_rows, slots = ck.shape[0], ck.shape[1]
    dr = drow * steps * groups
    fr = drow * steps
    nq = rows * mine
    nd = own_rows * steps * groups
    tiles = (nq + nd) // TILE
    half = n // 2
    bf = jnp.bfloat16
    dma = pltpu.SemaphoreType.DMA
    hbm = pl.BlockSpec(memory_space=pl.ANY)
    out, dec = pl.pallas_call(
        functools.partial(
            kernel, n, peers, slots, steps, groups, size**-0.5 * math.log2(math.e)
        ),
        out_shape=(
            jax.ShapeDtypeStruct((nq, size), bf),
            jax.ShapeDtypeStruct((heads, dr, size), bf),
        ),
        in_specs=[hbm] * 8 + [pl.BlockSpec(memory_space=pltpu.SMEM)],
        out_specs=(hbm, hbm),
        scratch_shapes=[
            pltpu.VMEM((n, 2, 2, 2, width, size), bf),
            pltpu.VMEM((tiles, size, TILE), bf),
            pltpu.VMEM((tiles, size + ONES, TILE), jnp.float32),
            pltpu.VMEM((tiles, 1, TILE), jnp.float32),
            pltpu.VMEM((peers, dr + 2 * fr, size), bf),
            pltpu.VMEM((peers, dr, size), bf),
            pltpu.VMEM((peers, dr, size), bf),
            pltpu.VMEM((own_rows, slots, size), bf),
            pltpu.VMEM((own_rows, slots, size), bf),
            pltpu.VMEM((nq, size), bf),
            pltpu.VMEM((width, size), bf),
            pltpu.VMEM((width, size), bf),
            pltpu.VMEM((fr, heads, groups, size), bf),
            pltpu.VMEM((fr, heads, size), bf),
            pltpu.VMEM((fr, heads, size), bf),
            pltpu.VMEM((peers, dr + 2 * fr, size), bf),
            pltpu.VMEM((4 * width, TILE), jnp.float32),
            pltpu.VMEM((4 * width, TILE), jnp.float32),
            pltpu.VMEM((1, TILE), jnp.float32),
            pltpu.VMEM((1, TILE), jnp.float32),
            pltpu.VMEM((nq, size), bf),
            dma((half + 1, 2, 2, 2)),
            dma((half + 1, 2, 2, 2)),
            dma((half + 1, 2, 2)),
            dma((half + 1, 2, 2)),
            dma((1,)),
            dma((1,)),
            dma((peers,)),
            dma((peers,)),
            dma((peers,)),
            dma((peers,)),
            dma((8,)),
        ],
        compiler_params=pltpu.CompilerParams(
            collective_id=0, has_side_effects=True, vmem_limit_bytes=60 * 1024 * 1024
        ),
        cost_estimate=pl.CostEstimate(
            flops=4 * (nq + nd) * n * 4 * width * size,
            bytes_accessed=8 * 1024 * 1024,
            transcendentals=(nq + nd) * n * 4 * width,
        ),
        name="shared_prompt_attention",
    )(
        pq.reshape(nq, size),
        pk.reshape(width, size),
        pv.reshape(width, size),
        dq.reshape(fr, heads, groups, size),
        nk.reshape(fr, heads, size),
        nv.reshape(fr, heads, size),
        ck.reshape(own_rows, slots, size),
        cv.reshape(own_rows, slots, size),
        lens,
    )
    decoded = jnp.moveaxis(dec.reshape(heads, drow, steps, groups, size), 0, 2)
    return out.reshape(pq.shape), decoded


def solution(mesh):
    return jax.shard_map(
        functools.partial(shards, mesh.shape["ctx"], mesh.shape["tp"]),
        mesh=mesh,
        in_specs=(
            P("ctx", "tp", "sec", None),
            P(("ctx", "sec"), "tp", None),
            P(("ctx", "sec"), "tp", None),
            P(("ctx", "sec", "tp"), None, None, None, None),
            P(("ctx", "sec", "tp"), None, None, None),
            P(("ctx", "sec", "tp"), None, None, None),
            P(("ctx", "sec"), None, "tp", None),
            P(("ctx", "sec"), None, "tp", None),
            P(("ctx", "sec")),
        ),
        out_specs=(P("ctx", "tp", "sec", None), P(("ctx", "sec", "tp"), None, None, None, None)),
        check_vma=False,
    )
```

```python
import functools
import math

import jax
import jax.numpy as jnp
from jax import lax
from jax.experimental import pallas as pl
from jax.experimental.pallas import tpu as pltpu
from jax.sharding import PartitionSpec as P

NEG = -1e30
MESH = pl.DeviceIdType.MESH
TILE = 512
ONES = 16


def kernel(
    n, peers, slots, steps, groups, scale2,
    pq_hbm, k_hbm, v_hbm, dq_hbm, nk_hbm, nv_hbm, ck_hbm, cv_hbm, lens_ref,
    out_hbm, dec_hbm,
    kv, qt, acc, top, inbox, outbox, back, ck, cv,
    pq_ref, k_ref, v_ref, dq, nk, nv, pack_ref, score_a, score_b, high_a, high_b,
    out_ref,
    ring_send, ring_recv, sib_send, sib_recv, y_send, y_recv,
    in_send, in_recv, out_send, out_recv, load_sem,
):
    i = lax.axis_index("ctx")
    sec = lax.axis_index("sec")
    tp = lax.axis_index("tp")
    half = n // 2
    h, c = sec // 2, lax.rem(sec, 2)
    right = lax.rem(i + 1, n)
    left = lax.rem(i + n - 1, n)
    to_right, to_left = (right, sec, tp), (left, sec, tp)
    sibling = (i, h * 2 + 1 - c, tp)
    across = (i, (1 - h) * 2 + c, tp)
    width = k_ref.shape[0]
    block = 4 * width
    ptiles = pq_ref.shape[0] // TILE
    dtiles = qt.shape[0] - ptiles
    drows = outbox.shape[1]
    srcs = TILE // drows

    barrier = pltpu.get_barrier_semaphore()
    for device in (to_right, to_left, sibling, across):
        pl.semaphore_signal(barrier, inc=1, device_id=device, device_id_type=MESH)
    for j in range(1, peers):
        device = (i, sec, lax.rem(tp + j, peers))
        pl.semaphore_signal(barrier, inc=1, device_id=device, device_id_type=MESH)

    sources = (k_hbm, v_hbm, dq_hbm, nk_hbm, nv_hbm, pq_hbm, ck_hbm, cv_hbm)
    targets = (k_ref, v_ref, dq, nk, nv, pq_ref, ck, cv)
    loads = [
        pltpu.make_async_copy(source, target, load_sem.at[at])
        for at, (source, target) in enumerate(zip(sources, targets))
    ]
    for load in loads:
        load.start()
    loads[0].wait()
    loads[1].wait()
    kv[i, c, h, 0] = k_ref[...]
    kv[i, c, h, 1] = v_ref[...].astype(jnp.float32).T.astype(jnp.bfloat16)
    pl.semaphore_wait(barrier, 3 + peers)

    sign = 1 - 2 * c
    onward = (jnp.where(c == 0, right, left), sec, tp)

    def mine(s):
        return lax.rem(i + n - s * sign, n)

    def theirs(s):
        return lax.rem(i + n + s * sign, n)

    def ring(s, cc, hh, w):
        return pltpu.make_async_remote_copy(
            src_ref=kv.at[mine(s), cc, hh, w],
            dst_ref=kv.at[mine(s), cc, hh, w],
            send_sem=ring_send.at[s, cc, hh, w],
            recv_sem=ring_recv.at[s + 1, cc, hh, w],
            device_id=onward,
            device_id_type=MESH,
        )

    def launch(s, cc, hh):
        for w in range(2):
            ring(s, cc, hh, w).start()

    def side(s, cc, hh, z=None):
        z = mine(s) if z is None else z
        return pltpu.make_async_remote_copy(
            src_ref=kv.at[z, cc, hh],
            dst_ref=kv.at[z, cc, hh],
            send_sem=sib_send.at[s, cc, hh],
            recv_sem=sib_recv.at[s, cc, hh],
            device_id=sibling,
            device_id_type=MESH,
        )

    def side_wait(s, cc, hh):
        side(s, cc, hh, theirs(s)).wait_recv()

    def landed(s, cc, hh, w):
        pltpu.make_async_remote_copy(
            src_ref=kv.at[mine(s), cc, hh, w],
            dst_ref=kv.at[mine(s), cc, hh, w],
            send_sem=ring_send.at[s - 1, cc, hh, w],
            recv_sem=ring_recv.at[s, cc, hh, w],
            device_id=onward,
            device_id_type=MESH,
        ).wait_recv()

    def cross(hh):
        return pltpu.make_async_remote_copy(
            src_ref=kv.at[i, c, hh],
            dst_ref=kv.at[i, c, hh],
            send_sem=y_send.at[0],
            recv_sem=y_recv.at[0],
            device_id=across,
            device_id_type=MESH,
        )

    def inward(j):
        to = lax.rem(tp + j, peers)
        return pltpu.make_async_remote_copy(
            src_ref=pack_ref.at[to],
            dst_ref=inbox.at[tp],
            send_sem=in_send.at[j],
            recv_sem=in_recv.at[j],
            device_id=(i, sec, to),
            device_id_type=MESH,
        )

    def inward_wait(j):
        source = lax.rem(tp + peers - j, peers)
        pltpu.make_async_remote_copy(
            src_ref=pack_ref.at[source],
            dst_ref=inbox.at[source],
            send_sem=in_send.at[j],
            recv_sem=in_recv.at[j],
            device_id=(i, sec, source),
            device_id_type=MESH,
        ).wait_recv()

    def outward(j):
        to = lax.rem(tp + j, peers)
        return pltpu.make_async_remote_copy(
            src_ref=outbox.at[to],
            dst_ref=back.at[tp],
            send_sem=out_send.at[j],
            recv_sem=out_recv.at[j],
            device_id=(i, sec, to),
            device_id_type=MESH,
        )

    def outward_wait(j):
        source = lax.rem(tp + peers - j, peers)
        pltpu.make_async_remote_copy(
            src_ref=outbox.at[source],
            dst_ref=back.at[source],
            send_sem=out_send.at[j],
            recv_sem=out_recv.at[j],
            device_id=(i, sec, source),
            device_id_type=MESH,
        ).wait_recv()

    launch(0, c, h)
    cross(h).start()
    side(0, c, h).start()
    for at in range(2, 5):
        loads[at].wait()
    queries = jnp.swapaxes(dq[...].astype(jnp.float32), 0, 1).reshape(peers, drows, -1)
    pack_ref[:, :drows, :] = queries.astype(jnp.bfloat16)
    pack_ref[:, drows:, :] = jnp.concatenate(
        [jnp.swapaxes(new[...].astype(jnp.float32), 0, 1) for new in (nk, nv)], axis=1
    ).astype(jnp.bfloat16)
    for j in range(1, peers):
        inward(j).start()
    inbox[tp] = pack_ref[tp]

    def turn_queries(rows):
        return rows.astype(jnp.float32).T.astype(jnp.bfloat16)

    def prepare(t, _):
        qt[t] = turn_queries(pq_ref[pl.ds(pl.multiple_of(t * TILE, TILE), TILE), :])
        return 0

    side_wait(0, 1 - c, h)
    launch(0, 1 - c, h)
    cross(1 - h).wait_recv()
    launch(0, c, 1 - h)
    side(0, c, 1 - h).start()
    side_wait(0, 1 - c, 1 - h)
    launch(0, 1 - c, 1 - h)
    loads[5].wait()
    lax.fori_loop(0, ptiles, prepare, 0)

    def advance(now, later, scores, high, scores_next, high_next, first, mask):
        z, t = now
        best = high[...]
        if not first:
            before = top[t]
            best = jnp.maximum(before, best)
        if later is not None:
            ahead(*later, scores_next, high_next, mask)
        weights = jnp.exp2((scores[...] - best) * scale2).astype(jnp.bfloat16)
        values = jnp.concatenate([kv[z, a, b, 1] for a in range(2) for b in range(2)], axis=1)
        values = jnp.concatenate([values, jnp.ones((ONES, block), jnp.bfloat16)], axis=0)
        mixed = jnp.dot(values, weights, preferred_element_type=jnp.float32)
        if not first:
            mixed = acc[t] * jnp.exp2((before - best) * scale2) + mixed
        acc[t] = mixed
        top[t] = best

    def ahead(z, t, scores, high, mask=None):
        keys = kv[z, :, :, 0].reshape(block, k_ref.shape[1])
        found = jnp.dot(keys, qt[t], preferred_element_type=jnp.float32)
        if mask is not None:
            found = jnp.where(mask(t), found, NEG)
        scores[...] = found
        high[...] = jnp.max(found, axis=0, keepdims=True)

    def lone(z, t, first=False):
        ahead(z, t, score_a, high_a)
        advance((z, t), None, score_a, high_a, None, None, first, None)

    def stream(count, item, first=False, mask=None, hook=None):
        def one(u, _):
            now, second = item(2 * u), item(2 * u + 1)
            later = item(jnp.minimum(2 * u + 2, count - 1))
            if hook is not None:
                pl.when(u == count // 4)(hook)
            advance(now, second, score_a, high_a, score_b, high_b, first, mask)
            advance(second, later, score_b, high_b, score_a, high_a, first, mask)
            return 0

        ahead(*item(0), score_a, high_a, mask)
        lax.fori_loop(0, count // 2, one, 0)

    def causal(t):
        slot = lax.broadcasted_iota(jnp.int32, (block, TILE), 0)
        core, upper = slot // (2 * width), lax.rem(slot // width, 2)
        position = (upper * 2 + core) * width + lax.rem(slot, width)
        query = (t * TILE + lax.broadcasted_iota(jnp.int32, (block, TILE), 1)) // 2
        return position <= query

    def relay(s, order):
        hh = h if order == 0 else 1 - h
        for cc in (c, 1 - c):
            for w in range(2):
                landed(s, cc, hh, w)

                @pl.when((s < half - 1) | (hh == c))
                def _():
                    ring(s, cc, hh, w).start()

            side(s, cc, hh).start()

    relay(jnp.int32(1), 0)
    stream(
        jnp.int32(ptiles), lambda e: (i, e), first=True, mask=causal,
        hook=lambda: relay(jnp.int32(1), 1),
    )

    for j in range(1, peers):
        inward_wait(j)
    for t in range(dtiles):
        rows = inbox[t * srcs : (t + 1) * srcs, :drows, :].reshape(TILE, -1)
        qt[ptiles + t] = turn_queries(rows)

    per = steps * groups
    own = 128 // per
    pairs = 128 // drows
    fresh = (inbox.shape[1] - drows) // 2

    def private(group):
        t, lanes = ptiles + group * 128 // TILE, pl.ds(group * 128 % TILE, 128)
        start = group * own
        queries = qt[t, :, lanes]
        lane_row = lax.broadcasted_iota(jnp.int32, (slots, 128), 1) // per
        limit = jnp.full((slots, 128), lens_ref[start], jnp.int32)
        s_cache = jnp.dot(ck[start], queries, preferred_element_type=jnp.float32)
        for r in range(1, own):
            found = jnp.dot(ck[start + r], queries, preferred_element_type=jnp.float32)
            s_cache = jnp.where(lane_row == r, found, s_cache)
            limit = jnp.where(lane_row == r, lens_ref[start + r], limit)
        slot = lax.broadcasted_iota(jnp.int32, (slots, 128), 0)
        s_cache = jnp.where(slot < limit, s_cache, NEG)
        source = group * pairs
        new_k = jnp.concatenate(
            [inbox[source + b, drows : drows + 2 * fresh, :] for b in range(pairs)], axis=0
        )
        s_new = jnp.dot(new_k, queries, preferred_element_type=jnp.float32)
        shape = (pairs * 2 * fresh, 128)
        key_id = lax.broadcasted_iota(jnp.int32, shape, 0)
        lane = lax.broadcasted_iota(jnp.int32, shape, 1)
        in_pair = lax.rem(key_id, 2 * fresh)
        key_row = key_id // (2 * fresh) * (fresh // steps) + in_pair // steps
        key_step = lax.rem(in_pair, steps)
        ok = (
            (in_pair < fresh)
            & (key_row == lane // per)
            & (key_step <= lax.rem(lane, per) // groups)
        )
        s_new = jnp.where(ok, s_new, NEG)
        before = top[t, :, lanes]
        best = jnp.maximum(
            jnp.max(s_cache, axis=0, keepdims=True), jnp.max(s_new, axis=0, keepdims=True)
        )
        best = jnp.maximum(before, best)
        w_cache = jnp.exp2((s_cache - best) * scale2)
        w_new = jnp.exp2((s_new - best) * scale2)
        sums = jnp.sum(w_cache, axis=0, keepdims=True) + jnp.sum(w_new, axis=0, keepdims=True)
        new_v = jnp.concatenate(
            [
                jnp.roll(
                    inbox[source + b, drows : drows + 2 * fresh, :].astype(jnp.float32),
                    -fresh,
                    axis=0,
                )
                for b in range(pairs)
            ],
            axis=0,
        ).astype(jnp.bfloat16)
        turned = w_cache.T.astype(jnp.bfloat16)
        mixed = jnp.concatenate(
            [
                jnp.dot(
                    turned[r * per : (r + 1) * per],
                    cv[start + r],
                    preferred_element_type=jnp.float32,
                )
                for r in range(own)
            ],
            axis=0,
        ).T + lax.dot_general(
            new_v,
            w_new.astype(jnp.bfloat16),
            (((0,), (0,)), ((), ())),
            preferred_element_type=jnp.float32,
        )
        mixed = jnp.concatenate([mixed, jnp.broadcast_to(sums, (ONES, 128))], axis=0)
        acc[t, :, lanes] = acc[t, :, lanes] * jnp.exp2((before - best) * scale2) + mixed
        top[t, :, lanes] = best

    for t in range(dtiles):
        lone(i, ptiles + t, first=True)
    tiles = ptiles + dtiles

    def work(s, hook=None):
        z_right, z_left = mine(s), theirs(s)
        for cc in range(2):
            for hh in range(2):
                side_wait(s, cc, hh)
        low_right = jnp.where(z_right < i, 0, ptiles)
        low_left = jnp.where(z_left < i, 0, ptiles)
        turn = tiles - low_right

        def item(e):
            rightward = e < turn
            z = jnp.where(rightward, z_right, z_left)
            t = jnp.where(rightward, low_right + e, low_left + e - turn)
            return z, t

        stream(turn + tiles - low_left, item, hook=hook)

    relay(jnp.int32(2), 0)
    work(jnp.int32(1), lambda: relay(jnp.int32(2), 1))
    for load in loads[6:]:
        load.wait()
    private_groups = dtiles * TILE // 128

    def step(s, _):
        relay(s, 0)
        relay(s, 1)
        for group in range(private_groups):
            pl.when(s == 3 + group)(functools.partial(private, group))
        work(s - 1)
        return 0

    lax.fori_loop(3, half, step, 0)

    work(jnp.int32(half - 1))
    for cc in range(2):
        for w in range(2):
            landed(half, cc, c, w)
        side(half, cc, c).start()
    for cc in range(2):
        side_wait(half, cc, 1 - c)
    z = lax.rem(i + half, n)
    for t in range(dtiles):
        lone(z, ptiles + t)

    depth = acc.shape[1] - ONES
    for t in range(dtiles):
        total = acc[ptiles + t, depth : depth + 1, :]
        rows = (acc[ptiles + t, :depth, :] / total).T.astype(jnp.bfloat16)
        outbox[t * srcs : (t + 1) * srcs] = rows.reshape(srcs, drows, -1)
    for j in range(1, peers):
        outward(j).start()
    back[tp] = outbox[tp]

    @pl.when(z < i)
    def _():
        stream(jnp.int32(ptiles), lambda e: (z, e))

    def finish(t, _):
        total = acc[t, depth : depth + 1, :]
        rows = (acc[t, :depth, :] / total).T.astype(jnp.bfloat16)
        out_ref[pl.ds(pl.multiple_of(t * TILE, TILE), TILE), :] = rows
        return 0

    lax.fori_loop(0, ptiles, finish, 0)
    store = pltpu.make_async_copy(out_ref, out_hbm, load_sem.at[0])
    store.start()

    cross(h).wait_send()
    for hh in range(2):
        side(0, c, hh).wait_send()
        for cc in range(2):
            for w in range(2):
                ring(0, cc, hh, w).wait_send()

    def drain(s, _):
        for hh in range(2):
            for cc in range(2):
                side(s, cc, hh).wait_send()

                @pl.when((s < half - 1) | (hh == c))
                def _():
                    for w in range(2):
                        ring(s, cc, hh, w).wait_send()

        return 0

    lax.fori_loop(1, half, drain, 0)
    for cc in range(2):
        side(half, cc, c).wait_send()
    for j in range(1, peers):
        inward(j).wait_send()
    for j in range(1, peers):
        outward_wait(j)
    give = pltpu.make_async_copy(back, dec_hbm, load_sem.at[1])
    give.start()
    for j in range(1, peers):
        outward(j).wait_send()
    store.wait()
    give.wait()


def shards(n, peers, pq, pk, pv, dq, nk, nv, ck, cv, lens):
    rows, _, mine, size = pq.shape
    width = pk.shape[0]
    drow, steps, heads, groups, _ = dq.shape
    own_rows, slots = ck.shape[0], ck.shape[1]
    dr = drow * steps * groups
    fr = drow * steps
    nq = rows * mine
    nd = own_rows * steps * groups
    tiles = (nq + nd) // TILE
    half = n // 2
    bf = jnp.bfloat16
    dma = pltpu.SemaphoreType.DMA
    hbm = pl.BlockSpec(memory_space=pl.ANY)
    out, dec = pl.pallas_call(
        functools.partial(
            kernel, n, peers, slots, steps, groups, size**-0.5 * math.log2(math.e)
        ),
        out_shape=(
            jax.ShapeDtypeStruct((nq, size), bf),
            jax.ShapeDtypeStruct((heads, dr, size), bf),
        ),
        in_specs=[hbm] * 8 + [pl.BlockSpec(memory_space=pltpu.SMEM)],
        out_specs=(hbm, hbm),
        scratch_shapes=[
            pltpu.VMEM((n, 2, 2, 2, width, size), bf),
            pltpu.VMEM((tiles, size, TILE), bf),
            pltpu.VMEM((tiles, size + ONES, TILE), jnp.float32),
            pltpu.VMEM((tiles, 1, TILE), jnp.float32),
            pltpu.VMEM((peers, dr + 2 * fr, size), bf),
            pltpu.VMEM((peers, dr, size), bf),
            pltpu.VMEM((peers, dr, size), bf),
            pltpu.VMEM((own_rows, slots, size), bf),
            pltpu.VMEM((own_rows, slots, size), bf),
            pltpu.VMEM((nq, size), bf),
            pltpu.VMEM((width, size), bf),
            pltpu.VMEM((width, size), bf),
            pltpu.VMEM((fr, heads, groups, size), bf),
            pltpu.VMEM((fr, heads, size), bf),
            pltpu.VMEM((fr, heads, size), bf),
            pltpu.VMEM((peers, dr + 2 * fr, size), bf),
            pltpu.VMEM((4 * width, TILE), jnp.float32),
            pltpu.VMEM((4 * width, TILE), jnp.float32),
            pltpu.VMEM((1, TILE), jnp.float32),
            pltpu.VMEM((1, TILE), jnp.float32),
            pltpu.VMEM((nq, size), bf),
            dma((half + 1, 2, 2, 2)),
            dma((half + 1, 2, 2, 2)),
            dma((half + 1, 2, 2)),
            dma((half + 1, 2, 2)),
            dma((1,)),
            dma((1,)),
            dma((peers,)),
            dma((peers,)),
            dma((peers,)),
            dma((peers,)),
            dma((8,)),
        ],
        compiler_params=pltpu.CompilerParams(
            collective_id=0, has_side_effects=True, vmem_limit_bytes=60 * 1024 * 1024
        ),
        cost_estimate=pl.CostEstimate(
            flops=4 * (nq + nd) * n * 4 * width * size,
            bytes_accessed=8 * 1024 * 1024,
            transcendentals=(nq + nd) * n * 4 * width,
        ),
        name="shared_prompt_attention",
    )(
        pq.reshape(nq, size),
        pk.reshape(width, size),
        pv.reshape(width, size),
        dq.reshape(fr, heads, groups, size),
        nk.reshape(fr, heads, size),
        nv.reshape(fr, heads, size),
        ck.reshape(own_rows, slots, size),
        cv.reshape(own_rows, slots, size),
        lens,
    )
    decoded = jnp.moveaxis(dec.reshape(heads, drow, steps, groups, size), 0, 2)
    return out.reshape(pq.shape), decoded


def solution(mesh):
    return jax.shard_map(
        functools.partial(shards, mesh.shape["ctx"], mesh.shape["tp"]),
        mesh=mesh,
        in_specs=(
            P("ctx", "tp", "sec", None),
            P(("ctx", "sec"), "tp", None),
            P(("ctx", "sec"), "tp", None),
            P(("ctx", "sec", "tp"), None, None, None, None),
            P(("ctx", "sec", "tp"), None, None, None),
            P(("ctx", "sec", "tp"), None, None, None),
            P(("ctx", "sec"), None, "tp", None),
            P(("ctx", "sec"), None, "tp", None),
            P(("ctx", "sec")),
        ),
        out_specs=(P("ctx", "tp", "sec", None), P(("ctx", "sec", "tp"), None, None, None, None)),
        check_vma=False,
    )
```
